32 devices in a mesh: groups: 2 (over x), tile: 16 (over z, y, core).
Axes of the slice: x: 2, y: 2, z: 4, core: 2. Of those that a mesh axis runs over, the one named last changes fastest.
Arguments:
- gauss_params: float32 [14, 524288], P(None, ('groups', 'tile')), parts along dimension 1
- wanted: int32 [32, 16, 1024], P(('groups', 'tile')), parts along dimension 0, may hold values from 0 to 16383, as said below
- depth_order: int32 [512, 1024], P(('groups', 'tile')), parts along dimension 0, may hold values from 0 to 16383, as said below
- block_count: int32 [512], P(('groups', 'tile')), parts along dimension 0, may hold values from 1 to 8, as said below
- image_grad: float32 [512, 3, 256], P(('groups', 'tile')), parts along dimension 0, may hold values from -6 to 6
Outputs:
- image: float32 [512, 3, 256], P(('groups', 'tile')), parts along dimension 0
- param_grads: float32 [14, 524288], P(None, ('groups', 'tile')), parts along dimension 1
The draws below stay inside these ranges and needn't reach their ends.
There are 2 independent parts, one for each index of `groups`. The reference program is written for one: setup_inputs(seed, part) draws one part's arguments, and reference() takes and returns one part's arrays. A program takes and returns all parts, laid end to end along the dimension named above; each array names one. Nothing has to cross between parts.
Inputs may be any that keep to these rules, and one draw needn't show every extreme that they name: `wanted`: for each source device, every one of its 16384 local rows is requested by exactly one device at exactly one position. `depth_order`: the lists of one device's 16 tiles together name every position of its received list exactly once. `block_count`: every device owns a tile with 8 blocks; entries of depth_order beyond a tile's block count are not read.
All inputs are finite; a program needn't handle non-finite values.
Results may differ from the reference program's by a relative error of at most 0.0003.
Values sent between devices are 32-bit elements; how exact they have to be, the bound alone decides.
No kernel may reach another device: no remote copies, remote signals or barrier semaphores. Data moves between devices by JAX's collectives and lax.ppermute only.
A program may use at most 192 MiB of HBM per device.

```python
import math
import jax
import jax.numpy as jnp
from jax import lax

TILES_DEV = 16
NB_MAX = 8
BLOCK = 128
PIX = 256
G_DEV = 16384
CAP = 1024
GAUSS = 262144
TILES = 256
SLOTS = 1024


def layout(key):
    owners = TILES // TILES_DEV
    row_keys = jax.random.split(jax.random.fold_in(key, 101), owners)
    list_keys = jax.random.split(jax.random.fold_in(key, 202), owners)
    row_perm = jax.vmap(lambda k: jax.random.permutation(k, G_DEV))(row_keys).astype(jnp.int32)
    list_perm = jax.vmap(lambda k: jax.random.permutation(k, G_DEV))(list_keys).astype(jnp.int32)
    return (row_perm, list_perm)


def invert(perm):
    counter = jnp.arange(G_DEV, dtype=jnp.int32)
    return jnp.zeros((G_DEV,), jnp.int32).at[perm].set(counter)


def draw_wanted(key, part):
    row_perm, list_perm = layout(key)
    owners = TILES // TILES_DEV
    return jnp.transpose(row_perm.reshape(owners, owners, CAP), (1, 0, 2)).astype(jnp.int32)


def draw_depth_order(key, part):
    row_perm, list_perm = layout(key)
    return list_perm.reshape(TILES, SLOTS).astype(jnp.int32)


def draw_gauss_params(key, part):
    row_perm, list_perm = layout(key)
    key = jax.random.fold_in(key, 7)
    keys = jax.random.split(key, 8)
    owners = TILES // TILES_DEV
    row_place = jax.vmap(invert)(row_perm)
    list_place = jax.vmap(invert)(list_perm)
    source = jnp.arange(owners, dtype=jnp.int32)[:, None]
    asker = row_place // CAP
    slot = source * CAP + row_place % CAP
    rank = list_place[asker, slot]
    tile = (asker * TILES_DEV + rank // SLOTS).reshape(-1)
    order = (rank % SLOTS).reshape(-1).astype(jnp.float32)
    depth = 3.0 + 3.0 * (order + jax.random.uniform(keys[0], (GAUSS,), jnp.float32)) / SLOTS
    pix_u = (16 * (tile % 64)).astype(jnp.float32) + jax.random.uniform(keys[1], (GAUSS,), jnp.float32, -2.0, 18.0)
    pix_v = (16 * (tile // 64)).astype(jnp.float32) + jax.random.uniform(keys[2], (GAUSS,), jnp.float32, -2.0, 18.0)
    across = (pix_u - 512.0) * depth / 1000.0
    down = (pix_v - 512.0) * depth / 1000.0
    log_scale = jax.random.uniform(keys[3], (3, GAUSS), jnp.float32, math.log(0.003), math.log(0.015))
    quat_real = jax.random.uniform(keys[4], (1, GAUSS), jnp.float32, 0.5, 1.5)
    quat_imag = 0.5 * jax.random.normal(keys[5], (3, GAUSS), jnp.float32)
    opacity = jax.random.uniform(keys[6], (1, GAUSS), jnp.float32, -5.5, -3.5)
    colour = jnp.clip(3.0 * jax.random.normal(keys[7], (3, GAUSS), jnp.float32), -12.0, 12.0)
    place = jnp.stack([across, down, depth])
    return jnp.concatenate([place, log_scale, quat_real, quat_imag, opacity, colour], axis=0)


def draw_block_count(key, part):
    key = jax.random.fold_in(key, 13)
    keys = jax.random.split(key, 5)
    owners = TILES // TILES_DEV
    dense = jnp.repeat(jax.random.randint(keys[0], (owners,), 0, 4) == 0, TILES_DEV)
    roll = jax.random.randint(keys[1], (TILES,), 0, 8)
    heavy = jnp.where(dense, roll < 6, roll < 1)
    upper = jax.random.randint(keys[2], (TILES,), NB_MAX // 2 + 1, NB_MAX + 1)
    light = jax.random.randint(keys[3], (TILES,), 1, NB_MAX // 2 + 1)
    count = jnp.where(heavy, upper, light)
    chosen = jax.random.randint(keys[4], (owners,), 0, TILES_DEV)
    tile = jnp.arange(TILES, dtype=jnp.int32)
    forced = tile % TILES_DEV == jnp.repeat(chosen, TILES_DEV)
    return jnp.where(forced, NB_MAX, count).astype(jnp.int32)


def level_of(stream_key, shape, cuts, low, top_value):
    def one(axis_at, parts):
        steps = jax.random.uniform(jax.random.fold_in(jax.random.fold_in(stream_key, 6), axis_at), (parts,), jnp.float32, low / len(cuts), top_value / len(cuts))
        return jnp.repeat(jnp.exp(steps), shape[axis_at] // parts).reshape((-1,) + (1,) * (len(shape) - axis_at - 1))

    factor_of = one(*cuts[0])
    for cut in cuts[1:]:
        factor_of = factor_of * one(*cut)
    return factor_of


def gaussian(own_key, extent, scale, bound, cuts=(), held_as=jnp.bfloat16):
    loudness = level_of(own_key, extent, cuts, -0.22, 0.18) if cuts else 1.0
    values = jax.random.normal(own_key, extent, jnp.float32) * scale * loudness
    return jnp.minimum(jnp.maximum(values, -bound), bound).astype(held_as)


def setup_inputs(seed: int = 0, part: int = 0) -> dict:
    arg_keys = jax.random.split(jax.random.key(seed), 6)
    part_splits = jax.random.split(jax.random.fold_in(arg_keys[5], part), 6)
    gauss_params = draw_gauss_params(jax.random.fold_in(jax.random.fold_in(arg_keys[5], part), 71), part)
    wanted = draw_wanted(jax.random.fold_in(jax.random.fold_in(arg_keys[5], part), 71), part)
    depth_order = draw_depth_order(jax.random.fold_in(jax.random.fold_in(arg_keys[5], part), 71), part)
    block_count = draw_block_count(jax.random.fold_in(jax.random.fold_in(arg_keys[5], part), 71), part)
    image_grad = gaussian(part_splits[4], (TILES, 3, PIX), 1.0, 6.0, ((0, 16),), jnp.float32)
    return dict(gauss_params=gauss_params, wanted=wanted, depth_order=depth_order, block_count=block_count, image_grad=image_grad)


focal = 1000.0
center_u = 512.0
center_v = 512.0
dilate = 0.3
tile_row = 64

def project(raw):
    pos_x, pos_y, depth = (raw[0], raw[1], raw[2])
    scale_x, scale_y, scale_z = (jnp.exp(raw[3]), jnp.exp(raw[4]), jnp.exp(raw[5]))
    norm_inv = 1.0 / jnp.sqrt(raw[6] * raw[6] + raw[7] * raw[7] + raw[8] * raw[8] + raw[9] * raw[9])
    q_real, q_one, q_two, q_three = (raw[6] * norm_inv, raw[7] * norm_inv, raw[8] * norm_inv, raw[9] * norm_inv)
    rot = [[1.0 - 2.0 * (q_two * q_two + q_three * q_three), 2.0 * (q_one * q_two - q_real * q_three), 2.0 * (q_one * q_three + q_real * q_two)], [2.0 * (q_one * q_two + q_real * q_three), 1.0 - 2.0 * (q_one * q_one + q_three * q_three), 2.0 * (q_two * q_three - q_real * q_one)], [2.0 * (q_one * q_three - q_real * q_two), 2.0 * (q_two * q_three + q_real * q_one), 1.0 - 2.0 * (q_one * q_one + q_two * q_two)]]
    scales = [scale_x, scale_y, scale_z]
    mixed = [[rot[i][k] * scales[k] for k in range(3)] for i in range(3)]
    cov = [[mixed[i][0] * mixed[j][0] + mixed[i][1] * mixed[j][1] + mixed[i][2] * mixed[j][2] for j in range(3)] for i in range(3)]
    jac_uu = focal / depth
    jac_uz = -focal * pos_x / (depth * depth)
    jac_vv = focal / depth
    jac_vz = -focal * pos_y / (depth * depth)
    upper = [jac_uu * cov[0][k] + jac_uz * cov[2][k] for k in range(3)]
    lower = [jac_vv * cov[1][k] + jac_vz * cov[2][k] for k in range(3)]
    first = upper[0] * jac_uu + upper[2] * jac_uz + dilate
    cross = upper[1] * jac_vv + upper[2] * jac_vz
    second = lower[1] * jac_vv + lower[2] * jac_vz + dilate
    det_inv = 1.0 / (first * second - cross * cross)
    return jnp.stack([focal * pos_x / depth + center_u, focal * pos_y / depth + center_v, second * det_inv, -cross * det_inv, first * det_inv, jax.nn.sigmoid(raw[10]), raw[11], raw[12], raw[13]])

def pixels(tile_ids):
    pixel = jnp.arange(256, dtype=jnp.int32)
    pixel_u = (16 * (tile_ids % tile_row))[:, None] + (pixel % 16)[None, :]
    pixel_v = (16 * (tile_ids // tile_row))[:, None] + (pixel // 16)[None, :]
    return (pixel_u.astype(jnp.float32) + 0.5, pixel_v.astype(jnp.float32) + 0.5)

def earlier_table(count):
    index = jnp.arange(count, dtype=jnp.int32)
    return (index[:, None] < index[None, :]).astype(jnp.float32)

def blend(trans, rows, pixel_u, pixel_v, alive):
    delta_u = pixel_u[:, :, None] - rows[0][:, None, :]
    delta_v = pixel_v[:, :, None] - rows[1][:, None, :]
    power = -0.5 * (rows[2][:, None, :] * delta_u * delta_u + rows[4][:, None, :] * delta_v * delta_v) - rows[3][:, None, :] * delta_u * delta_v
    alpha = rows[5][:, None, :] * jnp.exp(power) * alive[:, None, None]
    logs = jnp.log1p(-alpha)
    table = earlier_table(alpha.shape[2])
    before = jnp.exp(jnp.einsum('mpi,ik->mpk', logs, table, precision=lax.Precision.HIGHEST))
    weight = trans[:, :, None] * before * alpha
    contrib = jnp.einsum('mpk,cmk->mcp', weight, rows[6:9], precision=lax.Precision.HIGHEST)
    last_keep = before[:, :, -1] * (1.0 - alpha[:, :, -1])
    return (contrib, trans * last_keep)

def tile_image(item):
    tile_id, rows, count = item
    pixel_u, pixel_v = pixels(tile_id[None])
    alive = jnp.ones((1,), jnp.float32)

    def step(carry, index):

        def live(state):
            block = lax.dynamic_slice_in_dim(rows, index * BLOCK, BLOCK, 1)[:, None, :]
            contrib, trans_out = blend(state[0], block, pixel_u, pixel_v, alive)
            return (trans_out, state[1] + contrib)

        def dead(state):
            return (state[0], state[1])
        return (lax.cond(index < count, live, dead, carry), None)
    start = (jnp.ones((1, 256), jnp.float32), jnp.zeros((1, 3, 256), jnp.float32))
    final, _ = lax.scan(step, start, jnp.arange(NB_MAX, dtype=jnp.int32))
    return final[1][0]

def reference(gauss_params, wanted, depth_order, block_count, image_grad):
    source = depth_order // CAP
    within = depth_order % CAP
    owner = (jnp.arange(TILES, dtype=jnp.int32) // TILES_DEV)[:, None]
    local_row = wanted[owner, source, within]
    slot_gaussian = (source * G_DEV + local_row).astype(jnp.int32)
    tile_ids = jnp.arange(TILES, dtype=jnp.int32)

    def render(params):
        projected = project(params)
        rows = jnp.take(projected, slot_gaussian.reshape(-1), axis=1).reshape(9, TILES, SLOTS)
        rows = jnp.moveaxis(rows, 1, 0)
        return lax.map(jax.checkpoint(tile_image), (tile_ids, rows, block_count))
    image, pull = jax.vjp(render, gauss_params)
    return (image, pull(image_grad)[0])
```

```python
import jax
import jax.numpy as jnp
from jax import lax
from jax.experimental import pallas as pl
from jax.experimental.pallas import tpu as pltpu
from jax.sharding import PartitionSpec as P

BLOCK = 128
PIX = 256
LANES = 128
ROWS = 8
CHAN = 9
PARAMS = 14
FINE = 5

focal = 1000.0
center_u = 512.0
center_v = 512.0
dilate = 0.3
tile_row = 64
log_floor = -200.0
vmem_bytes = 56 * 1024 * 1024

f32 = jnp.float32
bf16 = jnp.bfloat16


def pieces(value, count):
    out = []
    for _ in range(count - 1):
        head = value.astype(bf16)
        out.append(head)
        value = value - head.astype(f32)
    out.append(value.astype(bf16))
    return out


def fill_table(read, table, table_low, fine):
    for c in range(CHAN):
        wide = jnp.concatenate([read(c, 0), read(c, 1)], axis=1)
        part = pieces(wide, 3 if c < fine else 2)
        rows = pl.ds(c * 64, 64)
        table[rows, 0:256] = part[0]
        table[rows, 256:512] = part[1]
        if c < fine:
            table_low[rows, :] = part[2]


def pick(index, table, table_low, fine):
    column = (index & 127) | ((index >> 13) << 7)
    row = (index >> 7) & 63
    places = lax.broadcasted_iota(jnp.int32, (256, 256), 0)
    chosen = (jnp.broadcast_to(column, (256, 256)) == places).astype(f32).astype(bf16)
    row_hit = jnp.broadcast_to(row, (64, 256)) == lax.broadcasted_iota(jnp.int32, (64, 256), 0)
    both = jnp.dot(
        table[...], jnp.concatenate([chosen, chosen], axis=0), preferred_element_type=f32
    )
    if fine:
        low = jnp.dot(table_low[...], chosen, preferred_element_type=f32)
    out = []
    for c in range(CHAN):
        mine = both[c * 64 : c * 64 + 64]
        if c < fine:
            mine = mine + low[c * 64 : c * 64 + 64]
        out.append(jnp.sum(jnp.where(row_hit, mine, 0.0), axis=0, keepdims=True))
    return out


def gather_all(index_ref, out_ref, table, table_low, fine):
    def step(t, carry):
        for half in range(ROWS // 2):
            index = jnp.concatenate(
                [index_ref[t, 2 * half : 2 * half + 1, :], index_ref[t, 2 * half + 1 : 2 * half + 2, :]],
                axis=1,
            )
            for c, line in enumerate(pick(index, table, table_low, fine)):
                out_ref[t, c, 2 * half : 2 * half + 1, :] = line[:, :LANES]
                out_ref[t, c, 2 * half + 1 : 2 * half + 2, :] = line[:, LANES:]
        return carry

    lax.fori_loop(0, index_ref.shape[0], step, 0)


def invert_kernel(index_ref, out_ref):
    place = lax.broadcasted_iota(jnp.int32, (LANES, LANES), 0)
    lane = lax.broadcasted_iota(jnp.int32, (LANES, LANES), 1).astype(f32)

    def step(t, total):
        for s in range(ROWS):
            line = index_ref[t, s : s + 1, :]
            row_hit = jnp.broadcast_to(line >> 7, (LANES, LANES)) == place
            column_hit = jnp.broadcast_to(line & 127, (LANES, LANES)) == place
            here = (t * ROWS + s).astype(f32)
            left = jnp.concatenate(
                [jnp.where(row_hit, here, 0.0).astype(bf16), jnp.where(row_hit, lane, 0.0).astype(bf16)],
                axis=0,
            )
            right = jnp.where(column_hit, 1.0, 0.0).astype(bf16)
            total = total + lax.dot_general(
                left, right, (((1,), (1,)), ((), ())), preferred_element_type=f32
            )
        return total

    total = lax.fori_loop(0, index_ref.shape[0], step, jnp.zeros((2 * LANES, LANES), f32))
    value = (total[:LANES] * float(LANES) + total[LANES:]).astype(jnp.int32)
    for t in range(index_ref.shape[0]):
        out_ref[t] = value[t * ROWS : t * ROWS + ROWS]


def project_core(raw):
    pos_x, pos_y, depth = (raw[0], raw[1], raw[2])
    scale_x, scale_y, scale_z = (jnp.exp(raw[3]), jnp.exp(raw[4]), jnp.exp(raw[5]))
    norm_inv = 1.0 / jnp.sqrt(raw[6] * raw[6] + raw[7] * raw[7] + raw[8] * raw[8] + raw[9] * raw[9])
    q_real, q_one, q_two, q_three = (
        raw[6] * norm_inv,
        raw[7] * norm_inv,
        raw[8] * norm_inv,
        raw[9] * norm_inv,
    )
    rot = [
        [
            1.0 - 2.0 * (q_two * q_two + q_three * q_three),
            2.0 * (q_one * q_two - q_real * q_three),
            2.0 * (q_one * q_three + q_real * q_two),
        ],
        [
            2.0 * (q_one * q_two + q_real * q_three),
            1.0 - 2.0 * (q_one * q_one + q_three * q_three),
            2.0 * (q_two * q_three - q_real * q_one),
        ],
        [
            2.0 * (q_one * q_three - q_real * q_two),
            2.0 * (q_two * q_three + q_real * q_one),
            1.0 - 2.0 * (q_one * q_one + q_two * q_two),
        ],
    ]
    scales = [scale_x, scale_y, scale_z]
    mixed = [[rot[i][k] * scales[k] for k in range(3)] for i in range(3)]
    cov = [
        [
            mixed[i][0] * mixed[j][0] + mixed[i][1] * mixed[j][1] + mixed[i][2] * mixed[j][2]
            for j in range(3)
        ]
        for i in range(3)
    ]
    depth_inv = 1.0 / depth
    jac_uu = focal * depth_inv
    jac_uz = -jac_uu * (pos_x * depth_inv)
    jac_vv = jac_uu
    jac_vz = -jac_uu * (pos_y * depth_inv)
    upper = [jac_uu * cov[0][k] + jac_uz * cov[2][k] for k in range(3)]
    lower = [jac_vv * cov[1][k] + jac_vz * cov[2][k] for k in range(3)]
    first = upper[0] * jac_uu + upper[2] * jac_uz + dilate
    cross = upper[1] * jac_vv + upper[2] * jac_vz
    second = lower[1] * jac_vv + lower[2] * jac_vz + dilate
    det_inv = 1.0 / (first * second - cross * cross)
    return [
        focal * pos_x * depth_inv + center_u,
        focal * pos_y * depth_inv + center_v,
        second * det_inv,
        -cross * det_inv,
        first * det_inv,
    ]


def sigmoid(x):
    return 1.0 / (1.0 + jnp.exp(-x))


def project_kernel(params_ref, out_ref, raw):
    def step(t, carry):
        for s in range(ROWS):
            raw[:, s, :] = params_ref[:, pl.ds(pl.multiple_of((t * ROWS + s) * LANES, LANES), LANES)]
        rows = project_core([raw[k] for k in range(10)])
        for c in range(5):
            out_ref[t, c] = rows[c]
        out_ref[t, 5] = sigmoid(raw[10])
        for c in range(3):
            out_ref[t, 6 + c] = raw[11 + c]
        return carry

    lax.fori_loop(0, out_ref.shape[0], step, 0)


def read_half(ref, c, half):
    groups = ref.shape[0] // 2
    return jnp.concatenate([ref[half * groups + q, c] for q in range(groups)], axis=0)


def gather_kernel(fine, index_ref, in_ref, out_ref, table, table_low):
    fill_table(lambda c, half: read_half(in_ref, c, half), table, table_low, fine)
    gather_all(index_ref, out_ref, table, table_low, fine)


def return_kernel(index_ref, grads_ref, params_ref, out_ref, table, table_low, summed, raw, stage):
    fill_table(lambda c, half: read_half(grads_ref, c, half), table, table_low, 0)
    gather_all(index_ref, summed, table, table_low, 0)

    def step(t, carry):
        for s in range(ROWS):
            raw[:, s, :] = params_ref[:, pl.ds(pl.multiple_of((t * ROWS + s) * LANES, LANES), LANES)]
        _, pull = jax.vjp(project_core, [raw[k] for k in range(10)])
        core = pull([summed[t, c] for c in range(5)])[0]
        for k in range(10):
            stage[k] = core[k]
        stage[10] = summed[t, 5] * sigmoid(-raw[10])
        for c in range(3):
            stage[11 + c] = summed[t, 6 + c]
        for s in range(ROWS):
            out_ref[:, pl.ds(pl.multiple_of((t * ROWS + s) * LANES, LANES), LANES)] = stage[:, s, :]
        return carry

    lax.fori_loop(0, grads_ref.shape[0], step, 0)


def scan_before(value, row):
    total = value
    for shift in (1, 2, 4):
        total = total * jnp.where(row >= shift, pltpu.roll(total, shift, 0), 1.0)
    before = jnp.where(row >= 1, pltpu.roll(total, 1, 0), 1.0)
    return before, total[ROWS - 1 : ROWS, :]


def scan_behind(gain, offset, row, incoming):
    for shift in (1, 2, 4):
        inside = row < ROWS - shift
        offset = offset + gain * jnp.where(inside, pltpu.roll(offset, ROWS - shift, 0), 0.0)
        gain = gain * jnp.where(inside, pltpu.roll(gain, ROWS - shift, 0), 1.0)
    value = offset + gain * incoming
    behind = jnp.where(row < ROWS - 1, pltpu.roll(value, ROWS - 1, 0), incoming)
    return behind, value[0:1, :]


def two_rows(value):
    head = value.astype(bf16)
    return head, (value - head.astype(f32)).astype(bf16)


def blend_kernel(
    count_ref,
    first_ref,
    slots_ref,
    upstream_ref,
    image_ref,
    grads_ref,
    features,
    basis,
    alpha_s,
    gc_s,
    weight_s,
    gain_s,
    offset_s,
    pair,
    moments,
    colour_grads,
):
    t = pl.program_id(0)
    tile = first_ref[0] + t
    count = count_ref[t]
    mid_u = ((tile % tile_row) * 16 + 8).astype(f32)
    mid_v = ((tile // tile_row) * 16 + 8).astype(f32)
    pixel = lax.broadcasted_iota(jnp.int32, (1, PIX), 1)
    x = (pixel & 15).astype(f32) - 7.5
    y = (pixel >> 4).astype(f32) - 7.5
    row = lax.broadcasted_iota(jnp.int32, (ROWS, PIX), 0)

    @pl.when(t == 0)
    def _():
        basis[...] = jnp.zeros_like(basis)
        features[...] = jnp.zeros_like(features)
        for k in range(3):
            for m, line in enumerate((jnp.ones_like(x), x, y, x * x, x * y, y * y)):
                basis[6 * k + m : 6 * k + m + 1, 0:PIX] = line

    monomials = jnp.concatenate(
        [jnp.ones_like(x), x, y, x * x, x * y, y * y, jnp.zeros((2, PIX), f32)], axis=0
    ).astype(bf16)
    up = upstream_ref[0]
    up_head = up.astype(bf16).astype(f32)
    up_tail = up - up_head
    basis[18:21, PIX:] = up_head
    basis[21:24, PIX:] = up_tail
    basis[24:27, PIX:] = up_head
    basis16 = basis[...].astype(bf16)
    up_both = jnp.concatenate([up_head, up_tail, jnp.zeros((2, PIX), f32)], axis=0).astype(bf16)

    off_u = mid_u - slots_ref[0, 0]
    off_v = mid_v - slots_ref[0, 1]
    con_a, con_b, con_c = (slots_ref[0, 2], slots_ref[0, 3], slots_ref[0, 4])
    log_op = jnp.maximum(jnp.log(slots_ref[0, 5]), log_floor)
    side_u = con_a * off_u + con_b * off_v
    side_v = con_b * off_u + con_c * off_v
    coefs = [
        log_op - 0.5 * (off_u * side_u + off_v * side_v),
        -side_u,
        -side_v,
        -0.5 * con_a,
        -con_b,
        -0.5 * con_c,
    ]
    for m, coef in enumerate(coefs):
        for k, part in enumerate(pieces(coef, 3)):
            features[:, 6 * k + m, :] = part.astype(f32)
    for c in range(3):
        head, tail = two_rows(slots_ref[0, 6 + c])
        features[:, 18 + c, :] = head.astype(f32)
        features[:, 21 + c, :] = head.astype(f32)
        features[:, 24 + c, :] = tail.astype(f32)
    image_ref[...] = jnp.zeros_like(image_ref)
    grads_ref[...] = jnp.zeros_like(grads_ref)
    moments[...] = jnp.zeros_like(moments)
    colour_grads[...] = jnp.zeros_like(colour_grads)

    def forward(b, carry):
        trans, image = carry
        block = features[b]
        both = lax.dot_general(
            block.astype(bf16), basis16, (((0,), (0,)), ((), ())), preferred_element_type=f32
        )
        prod = jnp.ones((ROWS, PIX), f32)
        ahead = jnp.zeros((ROWS, PIX), f32)
        local = []
        for i in range(BLOCK // ROWS):
            alpha = jnp.exp(both[i * ROWS : i * ROWS + ROWS, :PIX])
            gc = both[i * ROWS : i * ROWS + ROWS, PIX:]
            weight = prod * alpha
            ahead = ahead + weight * gc
            prod = prod - weight
            alpha_s[b, i] = alpha
            gc_s[b, i] = gc
            local.append(weight)
        gain_s[b] = prod
        offset_s[b] = ahead
        before, whole = scan_before(prod, row)
        before = before * trans
        heads, tails = [], []
        for i in range(BLOCK // ROWS):
            weight = local[i] * before
            weight_s[b, i] = weight
            head, tail = two_rows(weight)
            heads.append(head)
            tails.append(tail)
        w2 = jnp.concatenate(heads + tails, axis=0)
        head = block[18:21]
        tail = block[24:27]
        colour = jnp.concatenate(
            [
                jnp.concatenate([head, tail, jnp.zeros((2, BLOCK), f32)], axis=0),
                jnp.concatenate([head, jnp.zeros((5, BLOCK), f32)], axis=0),
            ],
            axis=1,
        ).astype(bf16)
        image = image + jnp.dot(colour, w2, preferred_element_type=f32)
        got = lax.dot_general(up_both, w2, (((1,), (1,)), ((), ())), preferred_element_type=f32)
        colour_grads[:, b, :] = got[0:3, :BLOCK] + got[0:3, BLOCK:] + got[3:6, :BLOCK]
        return (trans * whole, image)

    _, image = lax.fori_loop(
        0, count, forward, (jnp.ones((1, PIX), f32), jnp.zeros((ROWS, PIX), f32))
    )
    image_ref[0] = image[0:3] + image[3:6]

    def backward(step, incoming):
        b = count - 1 - step
        behind, start = scan_behind(gain_s[b], offset_s[b], row, incoming)
        heads, tails = [], []
        for i in reversed(range(BLOCK // ROWS)):
            diff = gc_s[b, i] - behind
            head, tail = two_rows(weight_s[b, i] * diff)
            heads.append(head)
            tails.append(tail)
            behind = behind + alpha_s[b, i] * diff
        h2 = jnp.concatenate(heads[::-1] + tails[::-1], axis=0)
        got = lax.dot_general(monomials, h2, (((1,), (1,)), ((), ())), preferred_element_type=f32)
        moments[:, b, :] = got[:, :BLOCK] + got[:, BLOCK:]
        return start

    lax.fori_loop(0, count, backward, jnp.zeros((1, PIX), f32))

    sum_h, sum_x, sum_y, sum_xx, sum_xy, sum_yy = [moments[m] for m in range(6)]
    sum_u = sum_x + off_u * sum_h
    sum_v = sum_y + off_v * sum_h
    grads_ref[0, 0] = con_a * sum_u + con_b * sum_v
    grads_ref[0, 1] = con_b * sum_u + con_c * sum_v
    grads_ref[0, 2] = -0.5 * (sum_xx + off_u * (sum_x + sum_u))
    grads_ref[0, 3] = -(sum_xy + off_v * sum_x + off_u * sum_v)
    grads_ref[0, 4] = -0.5 * (sum_yy + off_v * (sum_y + sum_v))
    grads_ref[0, 5] = sum_h
    for c in range(3):
        grads_ref[0, 6 + c] = colour_grads[c]


def params(**kw):
    return pltpu.CompilerParams(vmem_limit_bytes=vmem_bytes, **kw)


def local(gauss_params, wanted, depth_order, block_count, image_grad):
    peers = wanted.shape[1]
    capacity = wanted.shape[2]
    tiles_here, slots = depth_order.shape
    gauss_here = gauss_params.shape[1]
    lines = capacity // LANES
    groups = gauss_here // (ROWS * LANES)
    blocks = slots // BLOCK
    shape = (groups, CHAN, ROWS, LANES)
    index_shape = (groups, ROWS, LANES)
    tables = [
        pltpu.VMEM((CHAN * 64, 512), bf16),
        pltpu.VMEM((FINE * 64, 256), bf16),
    ]

    def exchange(value):
        if lines != ROWS:
            value = value.transpose(0, 2, 1, 3).reshape(peers, lines, CHAN, LANES).transpose(0, 2, 1, 3)
        value = lax.all_to_all(value, "tile", split_axis=0, concat_axis=0, tiled=True)
        if lines != ROWS:
            value = value.transpose(0, 2, 1, 3).reshape(groups, ROWS, CHAN, LANES).transpose(0, 2, 1, 3)
        return value

    def invert(index):
        return pl.pallas_call(
            invert_kernel,
            out_shape=jax.ShapeDtypeStruct(index_shape, jnp.int32),
            compiler_params=params(),
        )(index)

    def gather(index, value, fine):
        return pl.pallas_call(
            lambda *refs: gather_kernel(fine, *refs),
            out_shape=jax.ShapeDtypeStruct(shape, f32),
            scratch_shapes=tables,
            compiler_params=params(),
        )(index, value)

    asked = lax.all_to_all(
        wanted.reshape(peers, lines, LANES), "tile", split_axis=0, concat_axis=0, tiled=True
    ).reshape(index_shape)
    projected = pl.pallas_call(
        project_kernel,
        out_shape=jax.ShapeDtypeStruct(shape, f32),
        scratch_shapes=[pltpu.VMEM((PARAMS, ROWS, LANES), f32)],
        compiler_params=params(),
    )(gauss_params)
    order = (
        depth_order.reshape(tiles_here, blocks, ROWS, BLOCK // ROWS)
        .transpose(0, 1, 3, 2)
        .reshape(tiles_here, blocks, BLOCK)
    )
    order_back = invert(order)
    outgoing = gather(asked, projected, FINE)
    arrived = exchange(outgoing)
    asked_back = invert(asked)
    slots_in = gather(order, arrived, FINE)
    first_tile = (lax.axis_index("tile") * tiles_here).reshape(1).astype(jnp.int32)
    steps = BLOCK // ROWS
    image, slot_grads = pl.pallas_call(
        blend_kernel,
        grid=(tiles_here,),
        in_specs=[
            pl.BlockSpec(memory_space=pltpu.SMEM),
            pl.BlockSpec(memory_space=pltpu.SMEM),
            pl.BlockSpec((1, CHAN, blocks, BLOCK), lambda t: (t, 0, 0, 0)),
            pl.BlockSpec((1, 3, PIX), lambda t: (t, 0, 0)),
        ],
        out_specs=[
            pl.BlockSpec((1, 3, PIX), lambda t: (t, 0, 0)),
            pl.BlockSpec((1, CHAN, blocks, BLOCK), lambda t: (t, 0, 0, 0)),
        ],
        out_shape=[
            jax.ShapeDtypeStruct((tiles_here, 3, PIX), f32),
            jax.ShapeDtypeStruct((tiles_here, CHAN, blocks, BLOCK), f32),
        ],
        scratch_shapes=[
            pltpu.VMEM((blocks, 32, BLOCK), f32),
            pltpu.VMEM((32, 2 * PIX), f32),
            pltpu.VMEM((blocks, steps, ROWS, PIX), f32),
            pltpu.VMEM((blocks, steps, ROWS, PIX), f32),
            pltpu.VMEM((blocks, steps, ROWS, PIX), f32),
            pltpu.VMEM((blocks, ROWS, PIX), f32),
            pltpu.VMEM((blocks, ROWS, PIX), f32),
            pltpu.VMEM((8, 128), f32),
            pltpu.VMEM((8, blocks, BLOCK), f32),
            pltpu.VMEM((3, blocks, BLOCK), f32),
        ],
        compiler_params=params(),
    )(block_count, first_tile, slots_in, image_grad)
    returned = exchange(gather(order_back, slot_grads, 0))
    param_grads = pl.pallas_call(
        return_kernel,
        out_shape=jax.ShapeDtypeStruct(gauss_params.shape, f32),
        scratch_shapes=tables
        + [
            pltpu.VMEM(shape, f32),
            pltpu.VMEM((PARAMS, ROWS, LANES), f32),
            pltpu.VMEM((PARAMS, ROWS, LANES), f32),
        ],
        compiler_params=params(),
    )(asked_back, returned, gauss_params)
    return (image, param_grads)


def solution(mesh):
    placed = (
        P(None, ("groups", "tile")),
        P(("groups", "tile"), None, None),
        P(("groups", "tile"), None),
        P(("groups", "tile")),
        P(("groups", "tile"), None, None),
    )
    return jax.shard_map(
        local,
        mesh=mesh,
        in_specs=placed,
        out_specs=(P(("groups", "tile"), None, None), P(None, ("groups", "tile"))),
        check_vma=False,
    )
```

```python
import jax
import jax.numpy as jnp
from jax import lax
from jax.experimental import pallas as pl
from jax.experimental.pallas import tpu as pltpu
from jax.sharding import PartitionSpec as P

BLOCK = 128
PIX = 256
LANES = 128
ROWS = 8
CHAN = 9
PARAMS = 14
FINE = 5
WIDE = 4

focal = 1000.0
center_u = 512.0
center_v = 512.0
dilate = 0.3
tile_row = 64
log_floor = -200.0
vmem_bytes = 56 * 1024 * 1024

f32 = jnp.float32
bf16 = jnp.bfloat16


def pieces(value, count):
    out = []
    for _ in range(count - 1):
        head = value.astype(bf16)
        out.append(head)
        value = value - head.astype(f32)
    out.append(value.astype(bf16))
    return out


def fill_table(read, table, table_low, fine):
    for c in range(CHAN):
        wide = jnp.concatenate([read(c, 0), read(c, 1)], axis=1)
        part = pieces(wide, 3 if c < fine else 2)
        rows = pl.ds(c * 64, 64)
        table[rows, 0:256] = part[0]
        table[rows, 256:512] = part[1]
        if c < fine:
            table_low[rows, :] = part[2]


def pick(index, table, table_low, fine):
    column = (index & 127) | ((index >> 13) << 7)
    row = (index >> 7) & 63
    places = lax.broadcasted_iota(jnp.int32, (256, 256), 0)
    chosen = (jnp.broadcast_to(column, (256, 256)) == places).astype(f32).astype(bf16)
    row_hit = jnp.broadcast_to(row, (64, 256)) == lax.broadcasted_iota(jnp.int32, (64, 256), 0)
    both = jnp.dot(
        table[...], jnp.concatenate([chosen, chosen], axis=0), preferred_element_type=f32
    )
    if fine:
        low = jnp.dot(table_low[...], chosen, preferred_element_type=f32)
    out = []
    for c in range(CHAN):
        mine = both[c * 64 : c * 64 + 64]
        if c < fine:
            mine = mine + low[c * 64 : c * 64 + 64]
        out.append(jnp.sum(jnp.where(row_hit, mine, 0.0), axis=0, keepdims=True))
    return out


def gather_all(index_ref, out_ref, table, table_low, fine):
    def step(t, carry):
        for half in range(ROWS // 2):
            index = jnp.concatenate(
                [index_ref[t, 2 * half : 2 * half + 1, :], index_ref[t, 2 * half + 1 : 2 * half + 2, :]],
                axis=1,
            )
            for c, line in enumerate(pick(index, table, table_low, fine)):
                out_ref[t, c, 2 * half : 2 * half + 1, :] = line[:, :LANES]
                out_ref[t, c, 2 * half + 1 : 2 * half + 2, :] = line[:, LANES:]
        return carry

    lax.fori_loop(0, index_ref.shape[0], step, 0)


def invert_kernel(index_ref, out_ref):
    place = lax.broadcasted_iota(jnp.int32, (LANES, LANES), 0)
    lane = lax.broadcasted_iota(jnp.int32, (LANES, LANES), 1).astype(f32)

    def step(t, total):
        for s in range(ROWS):
            line = index_ref[t, s : s + 1, :]
            row_hit = jnp.broadcast_to(line >> 7, (LANES, LANES)) == place
            column_hit = jnp.broadcast_to(line & 127, (LANES, LANES)) == place
            here = (t * ROWS + s).astype(f32)
            left = jnp.concatenate(
                [jnp.where(row_hit, here, 0.0).astype(bf16), jnp.where(row_hit, lane, 0.0).astype(bf16)],
                axis=0,
            )
            right = jnp.where(column_hit, 1.0, 0.0).astype(bf16)
            total = total + lax.dot_general(
                left, right, (((1,), (1,)), ((), ())), preferred_element_type=f32
            )
        return total

    total = lax.fori_loop(0, index_ref.shape[0], step, jnp.zeros((2 * LANES, LANES), f32))
    value = (total[:LANES] * float(LANES) + total[LANES:]).astype(jnp.int32)
    for t in range(index_ref.shape[0]):
        out_ref[t] = value[t * ROWS : t * ROWS + ROWS]


def project_core(raw):
    pos_x, pos_y, depth = (raw[0], raw[1], raw[2])
    scale_x, scale_y, scale_z = (jnp.exp(raw[3]), jnp.exp(raw[4]), jnp.exp(raw[5]))
    norm_inv = 1.0 / jnp.sqrt(raw[6] * raw[6] + raw[7] * raw[7] + raw[8] * raw[8] + raw[9] * raw[9])
    q_real, q_one, q_two, q_three = (
        raw[6] * norm_inv,
        raw[7] * norm_inv,
        raw[8] * norm_inv,
        raw[9] * norm_inv,
    )
    rot = [
        [
            1.0 - 2.0 * (q_two * q_two + q_three * q_three),
            2.0 * (q_one * q_two - q_real * q_three),
            2.0 * (q_one * q_three + q_real * q_two),
        ],
        [
            2.0 * (q_one * q_two + q_real * q_three),
            1.0 - 2.0 * (q_one * q_one + q_three * q_three),
            2.0 * (q_two * q_three - q_real * q_one),
        ],
        [
            2.0 * (q_one * q_three - q_real * q_two),
            2.0 * (q_two * q_three + q_real * q_one),
            1.0 - 2.0 * (q_one * q_one + q_two * q_two),
        ],
    ]
    scales = [scale_x, scale_y, scale_z]
    mixed = [[rot[i][k] * scales[k] for k in range(3)] for i in range(3)]
    cov = [
        [
            mixed[i][0] * mixed[j][0] + mixed[i][1] * mixed[j][1] + mixed[i][2] * mixed[j][2]
            for j in range(3)
        ]
        for i in range(3)
    ]
    depth_inv = 1.0 / depth
    jac_uu = focal * depth_inv
    jac_uz = -jac_uu * (pos_x * depth_inv)
    jac_vv = jac_uu
    jac_vz = -jac_uu * (pos_y * depth_inv)
    upper = [jac_uu * cov[0][k] + jac_uz * cov[2][k] for k in range(3)]
    lower = [jac_vv * cov[1][k] + jac_vz * cov[2][k] for k in range(3)]
    first = upper[0] * jac_uu + upper[2] * jac_uz + dilate
    cross = upper[1] * jac_vv + upper[2] * jac_vz
    second = lower[1] * jac_vv + lower[2] * jac_vz + dilate
    det_inv = 1.0 / (first * second - cross * cross)
    return [
        focal * pos_x * depth_inv + center_u,
        focal * pos_y * depth_inv + center_v,
        second * det_inv,
        -cross * det_inv,
        first * det_inv,
    ]


def sigmoid(x):
    return 1.0 / (1.0 + jnp.exp(-x))


def project_kernel(params_ref, out_ref, raw):
    def step(t, carry):
        for s in range(ROWS):
            raw[:, s, :] = params_ref[:, pl.ds(pl.multiple_of((t * ROWS + s) * LANES, LANES), LANES)]
        rows = project_core([raw[k] for k in range(10)])
        for c in range(5):
            out_ref[t, c] = rows[c]
        out_ref[t, 5] = sigmoid(raw[10])
        for c in range(3):
            out_ref[t, 6 + c] = raw[11 + c]
        return carry

    lax.fori_loop(0, out_ref.shape[0], step, 0)


def read_half(ref, c, half):
    groups = ref.shape[0] // 2
    return jnp.concatenate([ref[half * groups + q, c] for q in range(groups)], axis=0)


def gather_kernel(fine, index_ref, in_ref, out_ref, table, table_low):
    fill_table(lambda c, half: read_half(in_ref, c, half), table, table_low, fine)
    gather_all(index_ref, out_ref, table, table_low, fine)


def return_kernel(index_ref, grads_ref, params_ref, out_ref, table, table_low, summed, raw, stage):
    fill_table(lambda c, half: read_half(grads_ref, c, half), table, table_low, 0)
    gather_all(index_ref, summed, table, table_low, 0)

    def step(t, carry):
        for s in range(ROWS):
            raw[:, s, :] = params_ref[:, pl.ds(pl.multiple_of((t * ROWS + s) * LANES, LANES), LANES)]
        _, pull = jax.vjp(project_core, [raw[k] for k in range(10)])
        core = pull([summed[t, c] for c in range(5)])[0]
        for k in range(10):
            stage[k] = core[k]
        stage[10] = summed[t, 5] * sigmoid(-raw[10])
        for c in range(3):
            stage[11 + c] = summed[t, 6 + c]
        for s in range(ROWS):
            out_ref[:, pl.ds(pl.multiple_of((t * ROWS + s) * LANES, LANES), LANES)] = stage[:, s, :]
        return carry

    lax.fori_loop(0, grads_ref.shape[0], step, 0)


def scan_before(value, row):
    total = value
    for shift in (1, 2, 4):
        total = total * jnp.where(row >= shift, pltpu.roll(total, shift, 0), 1.0)
    before = jnp.where(row >= 1, pltpu.roll(total, 1, 0), 1.0)
    return before, total[ROWS - 1 : ROWS, :]


def scan_behind(gain, offset, row, incoming):
    for shift in (1, 2, 4):
        inside = row < ROWS - shift
        offset = offset + gain * jnp.where(inside, pltpu.roll(offset, ROWS - shift, 0), 0.0)
        gain = gain * jnp.where(inside, pltpu.roll(gain, ROWS - shift, 0), 1.0)
    value = offset + gain * incoming
    behind = jnp.where(row < ROWS - 1, pltpu.roll(value, ROWS - 1, 0), incoming)
    return behind, value[0:1, :]


def two_rows(value):
    head = value.astype(bf16)
    return head, (value - head.astype(f32)).astype(bf16)


def split_stack(values):
    both = [two_rows(value) for value in values]
    return jnp.concatenate([head for head, _ in both] + [tail for _, tail in both], axis=0)


def blend_kernel(
    count_ref,
    first_ref,
    slots_ref,
    upstream_ref,
    image_ref,
    grads_ref,
    live,
    features,
    basis,
    up_rows,
    alpha_s,
    gc_s,
    gain_s,
    offset_s,
    image_s,
    moments,
    colour_grads,
):
    tiles, _, blocks, _ = slots_ref.shape
    steps = BLOCK // ROWS
    spare = tiles * blocks
    pixel = lax.broadcasted_iota(jnp.int32, (1, PIX), 1)
    x = (pixel & 15).astype(f32) - 7.5
    y = (pixel >> 4).astype(f32) - 7.5
    row = lax.broadcasted_iota(jnp.int32, (ROWS, PIX), 0)
    block_row = lax.broadcasted_iota(jnp.int32, (blocks, BLOCK), 0)
    six = jnp.concatenate([jnp.ones_like(x), x, y, x * x, x * y, y * y], axis=0)
    power_basis = jnp.concatenate([six, six, six, jnp.zeros((14, PIX), f32)], axis=0).astype(bf16)
    monomials = jnp.concatenate([six, jnp.zeros((2, PIX), f32)], axis=0).astype(bf16)

    def middle(t):
        tile = first_ref[0] + t
        return (
            ((tile % tile_row) * 16 + 8).astype(f32),
            ((tile // tile_row) * 16 + 8).astype(f32),
        )

    basis[...] = jnp.zeros_like(basis)
    features[pl.ds(spare, 1)] = jnp.zeros((1, 32, BLOCK), f32)
    features[:, 27:32, :] = jnp.zeros((spare + 1, 5, BLOCK), f32)
    up_rows[pl.ds(tiles, 1)] = jnp.zeros((1, ROWS, PIX), f32)
    image_s[...] = jnp.zeros_like(image_s)

    def prepare(t, total):
        up = upstream_ref[t]
        up_head = up.astype(bf16).astype(f32)
        up_tail = up - up_head
        basis[t, 18:21, :] = up_head
        basis[t, 21:24, :] = up_tail
        basis[t, 24:27, :] = up_head
        up_rows[t] = jnp.concatenate([up_head, up_tail, jnp.zeros((2, PIX), f32)], axis=0)
        mid_u, mid_v = middle(t)
        off_u = mid_u - slots_ref[t, 0]
        off_v = mid_v - slots_ref[t, 1]
        con_a, con_b, con_c = (slots_ref[t, 2], slots_ref[t, 3], slots_ref[t, 4])
        log_op = jnp.maximum(jnp.log(slots_ref[t, 5]), log_floor)
        side_u = con_a * off_u + con_b * off_v
        side_v = con_b * off_u + con_c * off_v
        coefs = [
            log_op - 0.5 * (off_u * side_u + off_v * side_v),
            -side_u,
            -side_v,
            -0.5 * con_a,
            -con_b,
            -0.5 * con_c,
        ]
        here = pl.ds(t * blocks, blocks)
        for m, coef in enumerate(coefs):
            for k, part in enumerate(pieces(coef, 3)):
                features[here, 6 * k + m, :] = part.astype(f32)
        for c in range(3):
            head, tail = two_rows(slots_ref[t, 6 + c])
            features[here, 18 + c, :] = head.astype(f32)
            features[here, 21 + c, :] = head.astype(f32)
            features[here, 24 + c, :] = tail.astype(f32)
        for b in range(blocks):
            live[total] = t * blocks + b
            total = total + (b < count_ref[t]).astype(jnp.int32)
        return total

    total = lax.fori_loop(0, tiles, prepare, jnp.int32(0))
    for k in range(WIDE):
        live[total + k] = spare
    rounds = (total + WIDE - 1) // WIDE

    def local_pass(k, carry):
        for w in range(WIDE):
            name = live[k * WIDE + w]
            block = features[name].astype(bf16)
            power = lax.dot_general(
                block, power_basis, (((0,), (0,)), ((), ())), preferred_element_type=f32
            )
            shade = lax.dot_general(
                block,
                basis[name // blocks].astype(bf16),
                (((0,), (0,)), ((), ())),
                preferred_element_type=f32,
            )
            prod = jnp.ones((ROWS, PIX), f32)
            ahead = jnp.zeros((ROWS, PIX), f32)
            for i in range(steps):
                alpha = jnp.exp(power[i * ROWS : i * ROWS + ROWS])
                gc = shade[i * ROWS : i * ROWS + ROWS]
                weight = prod * alpha
                ahead = ahead + weight * gc
                prod = prod - weight
                alpha_s[name, i] = alpha
                gc_s[name, i] = gc
            gain_s[name] = prod
            offset_s[name] = ahead
        return carry

    lax.fori_loop(0, rounds, local_pass, 0)

    def scan_pass(t, carry):
        trans = jnp.ones((1, PIX), f32)
        gains, offsets = [], []
        for b in range(blocks):
            name = t * blocks + b
            alive = b < count_ref[t]
            gains.append(jnp.where(alive, gain_s[name], 1.0))
            offsets.append(jnp.where(alive, offset_s[name], 0.0))
        for b in range(blocks):
            before, whole = scan_before(gains[b], row)
            gain_s[t * blocks + b] = before * trans
            trans = trans * whole
        incoming = jnp.zeros((1, PIX), f32)
        for b in reversed(range(blocks)):
            behind, incoming = scan_behind(gains[b], offsets[b], row, incoming)
            offset_s[t * blocks + b] = behind
        return carry

    lax.fori_loop(0, tiles, scan_pass, 0)

    def grad_pass(k, carry):
        for w in range(WIDE):
            name = live[k * WIDE + w]
            t, b = name // blocks, name % blocks
            prod = gain_s[name]
            weights = []
            for i in range(steps):
                weight = prod * alpha_s[name, i]
                prod = prod - weight
                weights.append(weight)
            behind = offset_s[name]
            hits = []
            for i in reversed(range(steps)):
                diff = gc_s[name, i] - behind
                hits.append(weights[i] * diff)
                behind = behind + alpha_s[name, i] * diff
            w2 = split_stack(weights)
            h2 = split_stack(hits[::-1])
            head = features[name, 18:21]
            tail = features[name, 24:27]
            colour = jnp.concatenate(
                [
                    jnp.concatenate([head, tail, jnp.zeros((2, BLOCK), f32)], axis=0),
                    jnp.concatenate([head, jnp.zeros((5, BLOCK), f32)], axis=0),
                ],
                axis=1,
            ).astype(bf16)
            image_s[t] += jnp.dot(colour, w2, preferred_element_type=f32)
            got = lax.dot_general(
                up_rows[t].astype(bf16), w2, (((1,), (1,)), ((), ())), preferred_element_type=f32
            )
            colour_grads[t, :, b, :] = got[0:3, :BLOCK] + got[0:3, BLOCK:] + got[3:6, :BLOCK]
            got = lax.dot_general(
                monomials, h2, (((1,), (1,)), ((), ())), preferred_element_type=f32
            )
            moments[t, :, b, :] = got[:, :BLOCK] + got[:, BLOCK:]
        return carry

    lax.fori_loop(0, rounds, grad_pass, 0)

    def finish(t, carry):
        image_ref[t] = image_s[t, 0:3] + image_s[t, 3:6]
        alive = block_row < count_ref[t]
        sum_h, sum_x, sum_y, sum_xx, sum_xy, sum_yy = [
            jnp.where(alive, moments[t, m], 0.0) for m in range(6)
        ]
        mid_u, mid_v = middle(t)
        off_u = mid_u - slots_ref[t, 0]
        off_v = mid_v - slots_ref[t, 1]
        con_a, con_b, con_c = (slots_ref[t, 2], slots_ref[t, 3], slots_ref[t, 4])
        sum_u = sum_x + off_u * sum_h
        sum_v = sum_y + off_v * sum_h
        grads_ref[t, 0] = con_a * sum_u + con_b * sum_v
        grads_ref[t, 1] = con_b * sum_u + con_c * sum_v
        grads_ref[t, 2] = -0.5 * (sum_xx + off_u * (sum_x + sum_u))
        grads_ref[t, 3] = -(sum_xy + off_v * sum_x + off_u * sum_v)
        grads_ref[t, 4] = -0.5 * (sum_yy + off_v * (sum_y + sum_v))
        grads_ref[t, 5] = sum_h
        for c in range(3):
            grads_ref[t, 6 + c] = jnp.where(alive, colour_grads[t, c], 0.0)
        return carry

    lax.fori_loop(0, tiles, finish, 0)


def params(**kw):
    return pltpu.CompilerParams(vmem_limit_bytes=vmem_bytes, **kw)


def local(gauss_params, wanted, depth_order, block_count, image_grad):
    peers = wanted.shape[1]
    capacity = wanted.shape[2]
    tiles_here, slots = depth_order.shape
    gauss_here = gauss_params.shape[1]
    lines = capacity // LANES
    groups = gauss_here // (ROWS * LANES)
    blocks = slots // BLOCK
    shape = (groups, CHAN, ROWS, LANES)
    index_shape = (groups, ROWS, LANES)
    tables = [
        pltpu.VMEM((CHAN * 64, 512), bf16),
        pltpu.VMEM((FINE * 64, 256), bf16),
    ]

    def exchange(value):
        if lines != ROWS:
            value = value.transpose(0, 2, 1, 3).reshape(peers, lines, CHAN, LANES).transpose(0, 2, 1, 3)
        value = lax.all_to_all(value, "tile", split_axis=0, concat_axis=0, tiled=True)
        if lines != ROWS:
            value = value.transpose(0, 2, 1, 3).reshape(groups, ROWS, CHAN, LANES).transpose(0, 2, 1, 3)
        return value

    def invert(index):
        return pl.pallas_call(
            invert_kernel,
            out_shape=jax.ShapeDtypeStruct(index_shape, jnp.int32),
            compiler_params=params(),
        )(index)

    def gather(index, value, fine):
        return pl.pallas_call(
            lambda *refs: gather_kernel(fine, *refs),
            out_shape=jax.ShapeDtypeStruct(shape, f32),
            scratch_shapes=tables,
            compiler_params=params(),
        )(index, value)

    asked = lax.all_to_all(
        wanted.reshape(peers, lines, LANES), "tile", split_axis=0, concat_axis=0, tiled=True
    ).reshape(index_shape)
    projected = pl.pallas_call(
        project_kernel,
        out_shape=jax.ShapeDtypeStruct(shape, f32),
        scratch_shapes=[pltpu.VMEM((PARAMS, ROWS, LANES), f32)],
        compiler_params=params(),
    )(gauss_params)
    order = (
        depth_order.reshape(tiles_here, blocks, ROWS, BLOCK // ROWS)
        .transpose(0, 1, 3, 2)
        .reshape(tiles_here, blocks, BLOCK)
    )
    order_back = invert(order)
    outgoing = gather(asked, projected, FINE)
    arrived = exchange(outgoing)
    asked_back = invert(asked)
    slots_in = gather(order, arrived, FINE)
    first_tile = (lax.axis_index("tile") * tiles_here).reshape(1).astype(jnp.int32)
    steps = BLOCK // ROWS
    spare = tiles_here * blocks
    image, slot_grads = pl.pallas_call(
        blend_kernel,
        in_specs=[
            pl.BlockSpec(memory_space=pltpu.SMEM),
            pl.BlockSpec(memory_space=pltpu.SMEM),
            pl.BlockSpec(memory_space=pltpu.VMEM),
            pl.BlockSpec(memory_space=pltpu.VMEM),
        ],
        out_shape=[
            jax.ShapeDtypeStruct((tiles_here, 3, PIX), f32),
            jax.ShapeDtypeStruct((tiles_here, CHAN, blocks, BLOCK), f32),
        ],
        scratch_shapes=[
            pltpu.SMEM((spare + WIDE,), jnp.int32),
            pltpu.VMEM((spare + 1, 32, BLOCK), f32),
            pltpu.VMEM((tiles_here + 1, 32, PIX), f32),
            pltpu.VMEM((tiles_here + 1, ROWS, PIX), f32),
            pltpu.VMEM((spare + 1, steps, ROWS, PIX), f32),
            pltpu.VMEM((spare + 1, steps, ROWS, PIX), f32),
            pltpu.VMEM((spare + 1, ROWS, PIX), f32),
            pltpu.VMEM((spare + 1, ROWS, PIX), f32),
            pltpu.VMEM((tiles_here + 1, ROWS, PIX), f32),
            pltpu.VMEM((tiles_here + 1, ROWS, blocks, BLOCK), f32),
            pltpu.VMEM((tiles_here + 1, 3, blocks, BLOCK), f32),
        ],
        compiler_params=params(),
    )(block_count, first_tile, slots_in, image_grad)
    returned = exchange(gather(order_back, slot_grads, 0))
    param_grads = pl.pallas_call(
        return_kernel,
        out_shape=jax.ShapeDtypeStruct(gauss_params.shape, f32),
        scratch_shapes=tables
        + [
            pltpu.VMEM(shape, f32),
            pltpu.VMEM((PARAMS, ROWS, LANES), f32),
            pltpu.VMEM((PARAMS, ROWS, LANES), f32),
        ],
        compiler_params=params(),
    )(asked_back, returned, gauss_params)
    return (image, param_grads)


def solution(mesh):
    placed = (
        P(None, ("groups", "tile")),
        P(("groups", "tile"), None, None),
        P(("groups", "tile"), None),
        P(("groups", "tile")),
        P(("groups", "tile"), None, None),
    )
    return jax.shard_map(
        local,
        mesh=mesh,
        in_specs=placed,
        out_specs=(P(("groups", "tile"), None, None), P(None, ("groups", "tile"))),
        check_vma=False,
    )
```

```python
import jax
import jax.numpy as jnp
from jax import lax
from jax.experimental import pallas as pl
from jax.experimental.pallas import tpu as pltpu
from jax.sharding import PartitionSpec as P

BLOCK = 128
PIX = 256
LANES = 128
ROWS = 8
CHAN = 9
PARAMS = 14
LANED = 3
FINE = 2
WIDE = 8

focal = 1000.0
center_u = 512.0
center_v = 512.0
dilate = 0.3
tile_row = 64
log_floor = -200.0
vmem_bytes = 56 * 1024 * 1024

f32 = jnp.float32
bf16 = jnp.bfloat16


def pieces(value, count):
    out = []
    for _ in range(count - 1):
        head = value.astype(bf16)
        out.append(head)
        value = value - head.astype(f32)
    out.append(value.astype(bf16))
    return out


def fill_table(read, table, table_low, fine):
    for c in range(CHAN - LANED):
        wide = jnp.concatenate([read(LANED + c, 0), read(LANED + c, 1)], axis=1)
        part = pieces(wide, 3 if c < fine else 2)
        rows = pl.ds(c * 64, 64)
        table[rows, 0:256] = part[0]
        table[rows, 256:512] = part[1]
        if c < fine:
            table_low[rows, :] = part[2]


def pick(index, table, table_low, fine):
    column = (index & 127) | ((index >> 13) << 7)
    row = (index >> 7) & 63
    places = lax.broadcasted_iota(jnp.int32, (256, 256), 0).astype(f32).astype(bf16)
    column = jnp.broadcast_to(column.astype(f32).astype(bf16), (256, 256))
    chosen = jnp.where(column == places, bf16(1), bf16(0))
    row_hit = jnp.broadcast_to(row, (64, 256)) == lax.broadcasted_iota(jnp.int32, (64, 256), 0)
    both = jnp.dot(
        table[...], jnp.concatenate([chosen, chosen], axis=0), preferred_element_type=f32
    )
    if fine:
        low = jnp.dot(table_low[...], chosen, preferred_element_type=f32)
    out = []
    for c in range(CHAN - LANED):
        mine = both[c * 64 : c * 64 + 64]
        if c < fine:
            mine = mine + low[c * 64 : c * 64 + 64]
        out.append(jnp.sum(jnp.where(row_hit, mine, 0.0), axis=0, keepdims=True))
    return out


def gather_all(index_ref, in_ref, out_ref, table, table_low, fine):
    groups = in_ref.shape[0]
    fill_table(lambda c, half: read_half(in_ref, c, half), table, table_low, fine)

    def step(t, carry):
        whole = index_ref[t]
        row, column = whole >> 7, whole & 127
        found = [jnp.zeros((ROWS, LANES), f32) for _ in range(LANED)]
        quarter = groups // (ROWS // 2)
        for half in range(ROWS // 2):
            for q in range(half * quarter, half * quarter + quarter):
                for s in range(ROWS):
                    hit = row == q * ROWS + s
                    for c in range(LANED):
                        line = jnp.broadcast_to(in_ref[q, c, s : s + 1, :], (ROWS, LANES))
                        found[c] = jnp.where(
                            hit, jnp.take_along_axis(line, column, axis=1), found[c]
                        )
            index = jnp.concatenate(
                [index_ref[t, 2 * half : 2 * half + 1, :], index_ref[t, 2 * half + 1 : 2 * half + 2, :]],
                axis=1,
            )
            for c, line in enumerate(pick(index, table, table_low, fine)):
                out_ref[t, LANED + c, 2 * half : 2 * half + 1, :] = line[:, :LANES]
                out_ref[t, LANED + c, 2 * half + 1 : 2 * half + 2, :] = line[:, LANES:]
        for c in range(LANED):
            out_ref[t, c] = found[c]
        return carry

    lax.fori_loop(0, index_ref.shape[0], step, 0)


def invert_kernel(index_ref, out_ref):
    place = lax.broadcasted_iota(jnp.int32, (LANES, LANES), 0)
    lane = lax.broadcasted_iota(jnp.int32, (LANES, LANES), 1).astype(f32)

    def step(t, total):
        for s in range(ROWS):
            line = index_ref[t, s : s + 1, :]
            row_hit = jnp.broadcast_to(line >> 7, (LANES, LANES)) == place
            column_hit = jnp.broadcast_to(line & 127, (LANES, LANES)) == place
            here = (t * ROWS + s).astype(f32)
            left = jnp.concatenate(
                [jnp.where(row_hit, here, 0.0).astype(bf16), jnp.where(row_hit, lane, 0.0).astype(bf16)],
                axis=0,
            )
            right = jnp.where(column_hit, 1.0, 0.0).astype(bf16)
            total = total + lax.dot_general(
                left, right, (((1,), (1,)), ((), ())), preferred_element_type=f32
            )
        return total

    total = lax.fori_loop(0, index_ref.shape[0], step, jnp.zeros((2 * LANES, LANES), f32))
    value = (total[:LANES] * float(LANES) + total[LANES:]).astype(jnp.int32)
    for t in range(index_ref.shape[0]):
        out_ref[t] = value[t * ROWS : t * ROWS + ROWS]


def project_core(raw):
    pos_x, pos_y, depth = (raw[0], raw[1], raw[2])
    scale_x, scale_y, scale_z = (jnp.exp(raw[3]), jnp.exp(raw[4]), jnp.exp(raw[5]))
    norm_inv = 1.0 / jnp.sqrt(raw[6] * raw[6] + raw[7] * raw[7] + raw[8] * raw[8] + raw[9] * raw[9])
    q_real, q_one, q_two, q_three = (
        raw[6] * norm_inv,
        raw[7] * norm_inv,
        raw[8] * norm_inv,
        raw[9] * norm_inv,
    )
    rot = [
        [
            1.0 - 2.0 * (q_two * q_two + q_three * q_three),
            2.0 * (q_one * q_two - q_real * q_three),
            2.0 * (q_one * q_three + q_real * q_two),
        ],
        [
            2.0 * (q_one * q_two + q_real * q_three),
            1.0 - 2.0 * (q_one * q_one + q_three * q_three),
            2.0 * (q_two * q_three - q_real * q_one),
        ],
        [
            2.0 * (q_one * q_three - q_real * q_two),
            2.0 * (q_two * q_three + q_real * q_one),
            1.0 - 2.0 * (q_one * q_one + q_two * q_two),
        ],
    ]
    scales = [scale_x, scale_y, scale_z]
    mixed = [[rot[i][k] * scales[k] for k in range(3)] for i in range(3)]
    cov = [
        [
            mixed[i][0] * mixed[j][0] + mixed[i][1] * mixed[j][1] + mixed[i][2] * mixed[j][2]
            for j in range(3)
        ]
        for i in range(3)
    ]
    depth_inv = 1.0 / depth
    jac_uu = focal * depth_inv
    jac_uz = -jac_uu * (pos_x * depth_inv)
    jac_vv = jac_uu
    jac_vz = -jac_uu * (pos_y * depth_inv)
    upper = [jac_uu * cov[0][k] + jac_uz * cov[2][k] for k in range(3)]
    lower = [jac_vv * cov[1][k] + jac_vz * cov[2][k] for k in range(3)]
    first = upper[0] * jac_uu + upper[2] * jac_uz + dilate
    cross = upper[1] * jac_vv + upper[2] * jac_vz
    second = lower[1] * jac_vv + lower[2] * jac_vz + dilate
    det_inv = 1.0 / (first * second - cross * cross)
    return [
        focal * pos_x * depth_inv + center_u,
        focal * pos_y * depth_inv + center_v,
        second * det_inv,
        -cross * det_inv,
        first * det_inv,
    ]


def sigmoid(x):
    return 1.0 / (1.0 + jnp.exp(-x))


def project_kernel(params_ref, out_ref, raw):
    def step(t, carry):
        for s in range(ROWS):
            raw[:, s, :] = params_ref[:, pl.ds(pl.multiple_of((t * ROWS + s) * LANES, LANES), LANES)]
        rows = project_core([raw[k] for k in range(10)])
        for c in range(5):
            out_ref[t, c] = rows[c]
        out_ref[t, 5] = sigmoid(raw[10])
        for c in range(3):
            out_ref[t, 6 + c] = raw[11 + c]
        return carry

    lax.fori_loop(0, out_ref.shape[0], step, 0)


def read_half(ref, c, half):
    groups = ref.shape[0] // 2
    return jnp.concatenate([ref[half * groups + q, c] for q in range(groups)], axis=0)


def gather_kernel(fine, index_ref, in_ref, out_ref, table, table_low):
    gather_all(index_ref, in_ref, out_ref, table, table_low, fine)


def return_kernel(index_ref, grads_ref, params_ref, out_ref, table, table_low, summed, raw, stage):
    gather_all(index_ref, grads_ref, summed, table, table_low, 0)

    def step(t, carry):
        for s in range(ROWS):
            raw[:, s, :] = params_ref[:, pl.ds(pl.multiple_of((t * ROWS + s) * LANES, LANES), LANES)]
        _, pull = jax.vjp(project_core, [raw[k] for k in range(10)])
        core = pull([summed[t, c] for c in range(5)])[0]
        for k in range(10):
            stage[k] = core[k]
        stage[10] = summed[t, 5] * sigmoid(-raw[10])
        for c in range(3):
            stage[11 + c] = summed[t, 6 + c]
        for s in range(ROWS):
            out_ref[:, pl.ds(pl.multiple_of((t * ROWS + s) * LANES, LANES), LANES)] = stage[:, s, :]
        return carry

    lax.fori_loop(0, grads_ref.shape[0], step, 0)


def scan_before(value, row):
    total = value
    for shift in (1, 2, 4):
        total = total * jnp.where(row >= shift, pltpu.roll(total, shift, 0), 1.0)
    before = jnp.where(row >= 1, pltpu.roll(total, 1, 0), 1.0)
    return before, total[ROWS - 1 : ROWS, :]


def scan_behind(gain, offset, row, incoming):
    for shift in (1, 2, 4):
        inside = row < ROWS - shift
        offset = offset + gain * jnp.where(inside, pltpu.roll(offset, ROWS - shift, 0), 0.0)
        gain = gain * jnp.where(inside, pltpu.roll(gain, ROWS - shift, 0), 1.0)
    value = offset + gain * incoming
    behind = jnp.where(row < ROWS - 1, pltpu.roll(value, ROWS - 1, 0), incoming)
    return behind, value[0:1, :]


def two_rows(value):
    head = value.astype(bf16)
    return head, (value - head.astype(f32)).astype(bf16)


def split_stack(values):
    both = [two_rows(value) for value in values]
    return jnp.concatenate([head for head, _ in both] + [tail for _, tail in both], axis=0)


def blend_kernel(
    count_ref,
    first_ref,
    order_ref,
    back_ref,
    arrived_ref,
    upstream_ref,
    image_ref,
    sent_ref,
    table,
    table_low,
    slots_ref,
    grads_ref,
    live,
    features,
    basis,
    up_rows,
    alpha_s,
    gc_s,
    gain_s,
    offset_s,
    image_s,
    moments,
    colour_grads,
):
    gather_all(order_ref, arrived_ref, slots_ref, table, table_low, FINE)
    tiles, _, blocks, _ = slots_ref.shape
    steps = BLOCK // ROWS
    spare = tiles * blocks
    pixel = lax.broadcasted_iota(jnp.int32, (1, PIX), 1)
    x = (pixel & 15).astype(f32) - 7.5
    y = (pixel >> 4).astype(f32) - 7.5
    row = lax.broadcasted_iota(jnp.int32, (ROWS, PIX), 0)
    block_row = lax.broadcasted_iota(jnp.int32, (blocks, BLOCK), 0)
    six = jnp.concatenate([jnp.ones_like(x), x, y, x * x, x * y, y * y], axis=0)
    power_basis = jnp.concatenate([six, six, six, jnp.zeros((14, PIX), f32)], axis=0).astype(bf16)
    monomials = jnp.concatenate([six, jnp.zeros((2, PIX), f32)], axis=0).astype(bf16)

    def middle(t):
        tile = first_ref[0] + t
        return (
            ((tile % tile_row) * 16 + 8).astype(f32),
            ((tile // tile_row) * 16 + 8).astype(f32),
        )

    basis[...] = jnp.zeros_like(basis)
    features[pl.ds(spare, 1)] = jnp.zeros((1, 32, BLOCK), f32)
    features[:, 27:32, :] = jnp.zeros((spare + 1, 5, BLOCK), f32)
    up_rows[pl.ds(tiles, 1)] = jnp.zeros((1, ROWS, PIX), f32)
    image_s[...] = jnp.zeros_like(image_s)

    def prepare(t, total):
        up = upstream_ref[t]
        up_head = up.astype(bf16).astype(f32)
        up_tail = up - up_head
        basis[t, 18:21, :] = up_head
        basis[t, 21:24, :] = up_tail
        basis[t, 24:27, :] = up_head
        up_rows[t] = jnp.concatenate([up_head, up_tail, jnp.zeros((2, PIX), f32)], axis=0)
        mid_u, mid_v = middle(t)
        off_u = mid_u - slots_ref[t, 0]
        off_v = mid_v - slots_ref[t, 1]
        con_a, con_b, con_c = (slots_ref[t, 2], slots_ref[t, 3], slots_ref[t, 4])
        log_op = jnp.maximum(jnp.log(slots_ref[t, 5]), log_floor)
        side_u = con_a * off_u + con_b * off_v
        side_v = con_b * off_u + con_c * off_v
        coefs = [
            log_op - 0.5 * (off_u * side_u + off_v * side_v),
            -side_u,
            -side_v,
            -0.5 * con_a,
            -con_b,
            -0.5 * con_c,
        ]
        here = pl.ds(t * blocks, blocks)
        for m, coef in enumerate(coefs):
            for k, part in enumerate(pieces(coef, 3)):
                features[here, 6 * k + m, :] = part.astype(f32)
        for c in range(3):
            head, tail = two_rows(slots_ref[t, 6 + c])
            features[here, 18 + c, :] = head.astype(f32)
            features[here, 21 + c, :] = head.astype(f32)
            features[here, 24 + c, :] = tail.astype(f32)
        for b in range(blocks):
            live[total] = t * blocks + b
            total = total + (b < count_ref[t]).astype(jnp.int32)
        return total

    total = lax.fori_loop(0, tiles, prepare, jnp.int32(0))
    for k in range(WIDE):
        live[total + k] = spare
    rounds = (total + WIDE - 1) // WIDE

    def local_pass(k, carry):
        for w in range(WIDE):
            name = live[k * WIDE + w]
            block = features[name].astype(bf16)
            power = lax.dot_general(
                block, power_basis, (((0,), (0,)), ((), ())), preferred_element_type=f32
            )
            shade = lax.dot_general(
                block,
                basis[name // blocks].astype(bf16),
                (((0,), (0,)), ((), ())),
                preferred_element_type=f32,
            )
            prod = jnp.ones((ROWS, PIX), f32)
            ahead = jnp.zeros((ROWS, PIX), f32)
            for i in range(steps):
                alpha = jnp.exp(power[i * ROWS : i * ROWS + ROWS])
                gc = shade[i * ROWS : i * ROWS + ROWS]
                weight = prod * alpha
                ahead = ahead + weight * gc
                prod = prod - weight
                alpha_s[name, i] = alpha
                gc_s[name, i] = gc
            gain_s[name] = prod
            offset_s[name] = ahead
        return carry

    lax.fori_loop(0, rounds, local_pass, 0)

    def scan_pass(t, carry):
        trans = jnp.ones((1, PIX), f32)
        gains, offsets = [], []
        for b in range(blocks):
            name = t * blocks + b
            alive = b < count_ref[t]
            gains.append(jnp.where(alive, gain_s[name], 1.0))
            offsets.append(jnp.where(alive, offset_s[name], 0.0))
        for b in range(blocks):
            before, whole = scan_before(gains[b], row)
            gain_s[t * blocks + b] = before * trans
            trans = trans * whole
        incoming = jnp.zeros((1, PIX), f32)
        for b in reversed(range(blocks)):
            behind, incoming = scan_behind(gains[b], offsets[b], row, incoming)
            offset_s[t * blocks + b] = behind
        return carry

    lax.fori_loop(0, tiles, scan_pass, 0)

    def grad_pass(k, carry):
        for w in range(WIDE):
            name = live[k * WIDE + w]
            t, b = name // blocks, name % blocks
            prod = gain_s[name]
            weights = []
            for i in range(steps):
                weight = prod * alpha_s[name, i]
                prod = prod - weight
                weights.append(weight)
            behind = offset_s[name]
            hits = []
            for i in reversed(range(steps)):
                diff = gc_s[name, i] - behind
                hits.append(weights[i] * diff)
                behind = behind + alpha_s[name, i] * diff
            w2 = split_stack(weights)
            h2 = split_stack(hits[::-1])
            head = features[name, 18:21]
            tail = features[name, 24:27]
            colour = jnp.concatenate(
                [
                    jnp.concatenate([head, tail, jnp.zeros((2, BLOCK), f32)], axis=0),
                    jnp.concatenate([head, jnp.zeros((5, BLOCK), f32)], axis=0),
                ],
                axis=1,
            ).astype(bf16)
            image_s[t] += jnp.dot(colour, w2, preferred_element_type=f32)
            got = lax.dot_general(
                up_rows[t].astype(bf16), w2, (((1,), (1,)), ((), ())), preferred_element_type=f32
            )
            colour_grads[t, :, b, :] = got[0:3, :BLOCK] + got[0:3, BLOCK:] + got[3:6, :BLOCK]
            got = lax.dot_general(
                monomials, h2, (((1,), (1,)), ((), ())), preferred_element_type=f32
            )
            moments[t, :, b, :] = got[:, :BLOCK] + got[:, BLOCK:]
        return carry

    lax.fori_loop(0, rounds, grad_pass, 0)

    def finish(t, carry):
        image_ref[t] = image_s[t, 0:3] + image_s[t, 3:6]
        alive = block_row < count_ref[t]
        sum_h, sum_x, sum_y, sum_xx, sum_xy, sum_yy = [
            jnp.where(alive, moments[t, m], 0.0) for m in range(6)
        ]
        mid_u, mid_v = middle(t)
        off_u = mid_u - slots_ref[t, 0]
        off_v = mid_v - slots_ref[t, 1]
        con_a, con_b, con_c = (slots_ref[t, 2], slots_ref[t, 3], slots_ref[t, 4])
        sum_u = sum_x + off_u * sum_h
        sum_v = sum_y + off_v * sum_h
        grads_ref[t, 0] = con_a * sum_u + con_b * sum_v
        grads_ref[t, 1] = con_b * sum_u + con_c * sum_v
        grads_ref[t, 2] = -0.5 * (sum_xx + off_u * (sum_x + sum_u))
        grads_ref[t, 3] = -(sum_xy + off_v * sum_x + off_u * sum_v)
        grads_ref[t, 4] = -0.5 * (sum_yy + off_v * (sum_y + sum_v))
        grads_ref[t, 5] = sum_h
        for c in range(3):
            grads_ref[t, 6 + c] = jnp.where(alive, colour_grads[t, c], 0.0)
        return carry

    lax.fori_loop(0, tiles, finish, 0)
    gather_all(back_ref, grads_ref, sent_ref, table, table_low, 0)


def params(**kw):
    return pltpu.CompilerParams(vmem_limit_bytes=vmem_bytes, **kw)


def local(gauss_params, wanted, depth_order, block_count, image_grad):
    peers = wanted.shape[1]
    capacity = wanted.shape[2]
    tiles_here, slots = depth_order.shape
    gauss_here = gauss_params.shape[1]
    lines = capacity // LANES
    groups = gauss_here // (ROWS * LANES)
    blocks = slots // BLOCK
    shape = (groups, CHAN, ROWS, LANES)
    index_shape = (groups, ROWS, LANES)
    tables = [
        pltpu.VMEM(((CHAN - LANED) * 64, 512), bf16),
        pltpu.VMEM((FINE * 64, 256), bf16),
    ]

    def exchange(value):
        if lines != ROWS:
            value = value.transpose(0, 2, 1, 3).reshape(peers, lines, CHAN, LANES).transpose(0, 2, 1, 3)
        value = lax.all_to_all(value, "tile", split_axis=0, concat_axis=0, tiled=True)
        if lines != ROWS:
            value = value.transpose(0, 2, 1, 3).reshape(groups, ROWS, CHAN, LANES).transpose(0, 2, 1, 3)
        return value

    def invert(index):
        return pl.pallas_call(
            invert_kernel,
            out_shape=jax.ShapeDtypeStruct(index_shape, jnp.int32),
            compiler_params=params(),
        )(index)

    def gather(index, value, fine):
        return pl.pallas_call(
            lambda *refs: gather_kernel(fine, *refs),
            out_shape=jax.ShapeDtypeStruct(shape, f32),
            scratch_shapes=tables,
            compiler_params=params(),
        )(index, value)

    asked = lax.all_to_all(
        wanted.reshape(peers, lines, LANES), "tile", split_axis=0, concat_axis=0, tiled=True
    ).reshape(index_shape)
    projected = pl.pallas_call(
        project_kernel,
        out_shape=jax.ShapeDtypeStruct(shape, f32),
        scratch_shapes=[pltpu.VMEM((PARAMS, ROWS, LANES), f32)],
        compiler_params=params(),
    )(gauss_params)
    order = (
        depth_order.reshape(tiles_here, blocks, ROWS, BLOCK // ROWS)
        .transpose(0, 1, 3, 2)
        .reshape(tiles_here, blocks, BLOCK)
    )
    order_back = invert(order)
    outgoing = gather(asked, projected, FINE)
    arrived = exchange(outgoing)
    asked_back = invert(asked)
    first_tile = (lax.axis_index("tile") * tiles_here).reshape(1).astype(jnp.int32)
    steps = BLOCK // ROWS
    spare = tiles_here * blocks
    image, sent = pl.pallas_call(
        blend_kernel,
        in_specs=[
            pl.BlockSpec(memory_space=pltpu.SMEM),
            pl.BlockSpec(memory_space=pltpu.SMEM),
            pl.BlockSpec(memory_space=pltpu.VMEM),
            pl.BlockSpec(memory_space=pltpu.VMEM),
            pl.BlockSpec(memory_space=pltpu.VMEM),
            pl.BlockSpec(memory_space=pltpu.VMEM),
        ],
        out_shape=[
            jax.ShapeDtypeStruct((tiles_here, 3, PIX), f32),
            jax.ShapeDtypeStruct(shape, f32),
        ],
        scratch_shapes=tables
        + [
            pltpu.VMEM((tiles_here, CHAN, blocks, BLOCK), f32),
            pltpu.VMEM((tiles_here, CHAN, blocks, BLOCK), f32),
            pltpu.SMEM((spare + WIDE,), jnp.int32),
            pltpu.VMEM((spare + 1, 32, BLOCK), f32),
            pltpu.VMEM((tiles_here + 1, 32, PIX), f32),
            pltpu.VMEM((tiles_here + 1, ROWS, PIX), f32),
            pltpu.VMEM((spare + 1, steps, ROWS, PIX), f32),
            pltpu.VMEM((spare + 1, steps, ROWS, PIX), f32),
            pltpu.VMEM((spare + 1, ROWS, PIX), f32),
            pltpu.VMEM((spare + 1, ROWS, PIX), f32),
            pltpu.VMEM((tiles_here + 1, ROWS, PIX), f32),
            pltpu.VMEM((tiles_here + 1, ROWS, blocks, BLOCK), f32),
            pltpu.VMEM((tiles_here + 1, 3, blocks, BLOCK), f32),
        ],
        compiler_params=params(),
    )(block_count, first_tile, order, order_back, arrived, image_grad)
    returned = exchange(sent)
    param_grads = pl.pallas_call(
        return_kernel,
        out_shape=jax.ShapeDtypeStruct(gauss_params.shape, f32),
        scratch_shapes=tables
        + [
            pltpu.VMEM(shape, f32),
            pltpu.VMEM((PARAMS, ROWS, LANES), f32),
            pltpu.VMEM((PARAMS, ROWS, LANES), f32),
        ],
        compiler_params=params(),
    )(asked_back, returned, gauss_params)
    return (image, param_grads)


def solution(mesh):
    placed = (
        P(None, ("groups", "tile")),
        P(("groups", "tile"), None, None),
        P(("groups", "tile"), None),
        P(("groups", "tile")),
        P(("groups", "tile"), None, None),
    )
    return jax.shard_map(
        local,
        mesh=mesh,
        in_specs=placed,
        out_specs=(P(("groups", "tile"), None, None), P(None, ("groups", "tile"))),
        check_vma=False,
    )
```

```python
import jax
import jax.numpy as jnp
from jax import lax
from jax.experimental import pallas as pl
from jax.experimental.pallas import tpu as pltpu
from jax.sharding import PartitionSpec as P

BLOCK = 128
PIX = 256
LANES = 128
ROWS = 8
CHAN = 9
PARAMS = 14
LANED = 3
AT_ONCE = 4
FINE = 2
WIDE = 8

focal = 1000.0
center_u = 512.0
center_v = 512.0
dilate = 0.3
tile_row = 64
log_floor = -200.0
vmem_bytes = 56 * 1024 * 1024

f32 = jnp.float32
bf16 = jnp.bfloat16


def pieces(value, count):
    out = []
    for _ in range(count - 1):
        head = value.astype(bf16)
        out.append(head)
        value = value - head.astype(f32)
    out.append(value.astype(bf16))
    return out


def fill_table(read, table, table_low, fine):
    for c in range(CHAN - LANED):
        wide = jnp.concatenate([read(LANED + c, 0), read(LANED + c, 1)], axis=1)
        part = pieces(wide, 3 if c < fine else 2)
        rows = pl.ds(c * 64, 64)
        table[rows, 0:256] = part[0]
        table[rows, 256:512] = part[1]
        if c < fine:
            table_low[rows, :] = part[2]


def pick(index, table, table_low, fine):
    column = (index & 127) | ((index >> 13) << 7)
    row = (index >> 7) & 63
    places = lax.broadcasted_iota(jnp.int32, (256, 256), 0).astype(f32).astype(bf16)
    column = jnp.broadcast_to(column.astype(f32).astype(bf16), (256, 256))
    chosen = jnp.where(column == places, bf16(1), bf16(0))
    row_hit = jnp.broadcast_to(row, (64, 256)) == lax.broadcasted_iota(jnp.int32, (64, 256), 0)
    both = jnp.dot(
        table[...], jnp.concatenate([chosen, chosen], axis=0), preferred_element_type=f32
    )
    if fine:
        low = jnp.dot(table_low[...], chosen, preferred_element_type=f32)
    out = []
    for c in range(CHAN - LANED):
        mine = both[c * 64 : c * 64 + 64]
        if c < fine:
            mine = mine + low[c * 64 : c * 64 + 64]
        out.append(jnp.sum(jnp.where(row_hit, mine, 0.0), axis=0, keepdims=True))
    return out


def gather_all(index_ref, in_ref, out_ref, table, table_low, fine, beside=None):
    groups = in_ref.shape[0]
    quarter = groups // (ROWS // 2)
    fill_table(lambda c, half: read_half(in_ref, c, half), table, table_low, fine)

    def one(t):
        whole = index_ref[t]
        row, column = whole >> 7, whole & 127
        found = [jnp.zeros((ROWS, LANES), f32) for _ in range(LANED)]
        for half in range(ROWS // 2):
            for q in range(half * quarter, half * quarter + quarter):
                for s in range(ROWS):
                    hit = row == q * ROWS + s
                    for c in range(LANED):
                        line = jnp.broadcast_to(in_ref[q, c, s : s + 1, :], (ROWS, LANES))
                        found[c] = jnp.where(
                            hit, jnp.take_along_axis(line, column, axis=1), found[c]
                        )
            index = jnp.concatenate(
                [index_ref[t, 2 * half : 2 * half + 1, :], index_ref[t, 2 * half + 1 : 2 * half + 2, :]],
                axis=1,
            )
            for c, line in enumerate(pick(index, table, table_low, fine)):
                out_ref[t, LANED + c, 2 * half : 2 * half + 1, :] = line[:, :LANES]
                out_ref[t, LANED + c, 2 * half + 1 : 2 * half + 2, :] = line[:, LANES:]
        for c in range(LANED):
            out_ref[t, c] = found[c]

    def step(k, carry):
        for u in range(AT_ONCE):
            if beside is not None:
                beside(jnp.maximum(k - 1, 0) * AT_ONCE + u)
        for u in range(AT_ONCE):
            one(k * AT_ONCE + u)
        return carry

    if beside is not None:
        for u in range(AT_ONCE):
            out_ref[u] = jnp.zeros_like(out_ref[u])
    lax.fori_loop(0, groups // AT_ONCE, step, 0)
    if beside is not None:
        for u in range(AT_ONCE):
            beside(groups - AT_ONCE + u)


def invert_kernel(index_ref, out_ref):
    place = lax.broadcasted_iota(jnp.int32, (LANES, LANES), 0)
    lane = lax.broadcasted_iota(jnp.int32, (LANES, LANES), 1).astype(f32)

    def step(t, total):
        for s in range(ROWS):
            line = index_ref[t, s : s + 1, :]
            row_hit = jnp.broadcast_to(line >> 7, (LANES, LANES)) == place
            column_hit = jnp.broadcast_to(line & 127, (LANES, LANES)) == place
            here = (t * ROWS + s).astype(f32)
            left = jnp.concatenate(
                [jnp.where(row_hit, here, 0.0).astype(bf16), jnp.where(row_hit, lane, 0.0).astype(bf16)],
                axis=0,
            )
            right = jnp.where(column_hit, 1.0, 0.0).astype(bf16)
            total = total + lax.dot_general(
                left, right, (((1,), (1,)), ((), ())), preferred_element_type=f32
            )
        return total

    total = lax.fori_loop(0, index_ref.shape[0], step, jnp.zeros((2 * LANES, LANES), f32))
    value = (total[:LANES] * float(LANES) + total[LANES:]).astype(jnp.int32)
    for t in range(index_ref.shape[0]):
        out_ref[t] = value[t * ROWS : t * ROWS + ROWS]


def project_core(raw):
    pos_x, pos_y, depth = (raw[0], raw[1], raw[2])
    scale_x, scale_y, scale_z = (jnp.exp(raw[3]), jnp.exp(raw[4]), jnp.exp(raw[5]))
    norm_inv = 1.0 / jnp.sqrt(raw[6] * raw[6] + raw[7] * raw[7] + raw[8] * raw[8] + raw[9] * raw[9])
    q_real, q_one, q_two, q_three = (
        raw[6] * norm_inv,
        raw[7] * norm_inv,
        raw[8] * norm_inv,
        raw[9] * norm_inv,
    )
    rot = [
        [
            1.0 - 2.0 * (q_two * q_two + q_three * q_three),
            2.0 * (q_one * q_two - q_real * q_three),
            2.0 * (q_one * q_three + q_real * q_two),
        ],
        [
            2.0 * (q_one * q_two + q_real * q_three),
            1.0 - 2.0 * (q_one * q_one + q_three * q_three),
            2.0 * (q_two * q_three - q_real * q_one),
        ],
        [
            2.0 * (q_one * q_three - q_real * q_two),
            2.0 * (q_two * q_three + q_real * q_one),
            1.0 - 2.0 * (q_one * q_one + q_two * q_two),
        ],
    ]
    scales = [scale_x, scale_y, scale_z]
    mixed = [[rot[i][k] * scales[k] for k in range(3)] for i in range(3)]
    cov = [
        [
            mixed[i][0] * mixed[j][0] + mixed[i][1] * mixed[j][1] + mixed[i][2] * mixed[j][2]
            for j in range(3)
        ]
        for i in range(3)
    ]
    depth_inv = 1.0 / depth
    jac_uu = focal * depth_inv
    jac_uz = -jac_uu * (pos_x * depth_inv)
    jac_vv = jac_uu
    jac_vz = -jac_uu * (pos_y * depth_inv)
    upper = [jac_uu * cov[0][k] + jac_uz * cov[2][k] for k in range(3)]
    lower = [jac_vv * cov[1][k] + jac_vz * cov[2][k] for k in range(3)]
    first = upper[0] * jac_uu + upper[2] * jac_uz + dilate
    cross = upper[1] * jac_vv + upper[2] * jac_vz
    second = lower[1] * jac_vv + lower[2] * jac_vz + dilate
    det_inv = 1.0 / (first * second - cross * cross)
    return [
        focal * pos_x * depth_inv + center_u,
        focal * pos_y * depth_inv + center_v,
        second * det_inv,
        -cross * det_inv,
        first * det_inv,
    ]


def sigmoid(x):
    return 1.0 / (1.0 + jnp.exp(-x))


def project_kernel(params_ref, out_ref, raw):
    def step(t, carry):
        for s in range(ROWS):
            raw[:, s, :] = params_ref[:, pl.ds(pl.multiple_of((t * ROWS + s) * LANES, LANES), LANES)]
        rows = project_core([raw[k] for k in range(10)])
        for c in range(5):
            out_ref[t, c] = rows[c]
        out_ref[t, 5] = sigmoid(raw[10])
        for c in range(3):
            out_ref[t, 6 + c] = raw[11 + c]
        return carry

    lax.fori_loop(0, out_ref.shape[0], step, 0)


def read_half(ref, c, half):
    groups = ref.shape[0] // 2
    return jnp.concatenate([ref[half * groups + q, c] for q in range(groups)], axis=0)


def gather_kernel(fine, index_ref, in_ref, out_ref, table, table_low):
    gather_all(index_ref, in_ref, out_ref, table, table_low, fine)


def return_kernel(index_ref, grads_ref, params_ref, out_ref, table, table_low, summed, raw, stage):
    def back(t):
        for s in range(ROWS):
            raw[:, s, :] = params_ref[:, pl.ds(pl.multiple_of((t * ROWS + s) * LANES, LANES), LANES)]
        _, pull = jax.vjp(project_core, [raw[k] for k in range(10)])
        core = pull([summed[t, c] for c in range(5)])[0]
        for k in range(10):
            stage[k] = core[k]
        stage[10] = summed[t, 5] * sigmoid(-raw[10])
        for c in range(3):
            stage[11 + c] = summed[t, 6 + c]
        for s in range(ROWS):
            out_ref[:, pl.ds(pl.multiple_of((t * ROWS + s) * LANES, LANES), LANES)] = stage[:, s, :]

    gather_all(index_ref, grads_ref, summed, table, table_low, 0, back)


def scan_before(value, row):
    total = value
    for shift in (1, 2, 4):
        total = total * jnp.where(row >= shift, pltpu.roll(total, shift, 0), 1.0)
    before = jnp.where(row >= 1, pltpu.roll(total, 1, 0), 1.0)
    return before, total[ROWS - 1 : ROWS, :]


def scan_behind(gain, offset, row, incoming):
    for shift in (1, 2, 4):
        inside = row < ROWS - shift
        offset = offset + gain * jnp.where(inside, pltpu.roll(offset, ROWS - shift, 0), 0.0)
        gain = gain * jnp.where(inside, pltpu.roll(gain, ROWS - shift, 0), 1.0)
    value = offset + gain * incoming
    behind = jnp.where(row < ROWS - 1, pltpu.roll(value, ROWS - 1, 0), incoming)
    return behind, value[0:1, :]


def two_rows(value):
    head = value.astype(bf16)
    return head, (value - head.astype(f32)).astype(bf16)


def split_stack(values):
    both = [two_rows(value) for value in values]
    return jnp.concatenate([head for head, _ in both] + [tail for _, tail in both], axis=0)


def blend_kernel(
    count_ref,
    first_ref,
    order_ref,
    back_ref,
    arrived_ref,
    upstream_ref,
    image_ref,
    sent_ref,
    table,
    table_low,
    slots_ref,
    grads_ref,
    live,
    features,
    basis,
    up_rows,
    alpha_s,
    gc_s,
    gain_s,
    offset_s,
    image_s,
    moments,
    colour_grads,
):
    gather_all(order_ref, arrived_ref, slots_ref, table, table_low, FINE)
    tiles, _, blocks, _ = slots_ref.shape
    steps = BLOCK // ROWS
    spare = tiles * blocks
    pixel = lax.broadcasted_iota(jnp.int32, (1, PIX), 1)
    x = (pixel & 15).astype(f32) - 7.5
    y = (pixel >> 4).astype(f32) - 7.5
    row = lax.broadcasted_iota(jnp.int32, (ROWS, PIX), 0)
    block_row = lax.broadcasted_iota(jnp.int32, (blocks, BLOCK), 0)
    six = jnp.concatenate([jnp.ones_like(x), x, y, x * x, x * y, y * y], axis=0)
    power_basis = jnp.concatenate([six, six, six, jnp.zeros((14, PIX), f32)], axis=0).astype(bf16)
    monomials = jnp.concatenate([six, jnp.zeros((2, PIX), f32)], axis=0).astype(bf16)

    def middle(t):
        tile = first_ref[0] + t
        return (
            ((tile % tile_row) * 16 + 8).astype(f32),
            ((tile // tile_row) * 16 + 8).astype(f32),
        )

    basis[...] = jnp.zeros_like(basis)
    features[pl.ds(spare, 1)] = jnp.zeros((1, 32, BLOCK), f32)
    features[:, 27:32, :] = jnp.zeros((spare + 1, 5, BLOCK), f32)
    up_rows[pl.ds(tiles, 1)] = jnp.zeros((1, ROWS, PIX), f32)
    image_s[...] = jnp.zeros_like(image_s)

    def prepare(t, total):
        up = upstream_ref[t]
        up_head = up.astype(bf16).astype(f32)
        up_tail = up - up_head
        basis[t, 18:21, :] = up_head
        basis[t, 21:24, :] = up_tail
        basis[t, 24:27, :] = up_head
        up_rows[t] = jnp.concatenate([up_head, up_tail, jnp.zeros((2, PIX), f32)], axis=0)
        mid_u, mid_v = middle(t)
        off_u = mid_u - slots_ref[t, 0]
        off_v = mid_v - slots_ref[t, 1]
        con_a, con_b, con_c = (slots_ref[t, 2], slots_ref[t, 3], slots_ref[t, 4])
        log_op = jnp.maximum(jnp.log(slots_ref[t, 5]), log_floor)
        side_u = con_a * off_u + con_b * off_v
        side_v = con_b * off_u + con_c * off_v
        coefs = [
            log_op - 0.5 * (off_u * side_u + off_v * side_v),
            -side_u,
            -side_v,
            -0.5 * con_a,
            -con_b,
            -0.5 * con_c,
        ]
        here = pl.ds(t * blocks, blocks)
        for m, coef in enumerate(coefs):
            for k, part in enumerate(pieces(coef, 3)):
                features[here, 6 * k + m, :] = part.astype(f32)
        for c in range(3):
            head, tail = two_rows(slots_ref[t, 6 + c])
            features[here, 18 + c, :] = head.astype(f32)
            features[here, 21 + c, :] = head.astype(f32)
            features[here, 24 + c, :] = tail.astype(f32)
        for b in range(blocks):
            live[total] = t * blocks + b
            total = total + (b < count_ref[t]).astype(jnp.int32)
        return total

    total = lax.fori_loop(0, tiles, prepare, jnp.int32(0), unroll=2)
    for k in range(WIDE):
        live[total + k] = spare
    rounds = (total + WIDE - 1) // WIDE

    def local_pass(k, carry):
        for w in range(WIDE):
            name = live[k * WIDE + w]
            block = features[name].astype(bf16)
            power = lax.dot_general(
                block, power_basis, (((0,), (0,)), ((), ())), preferred_element_type=f32
            )
            shade = lax.dot_general(
                block,
                basis[name // blocks].astype(bf16),
                (((0,), (0,)), ((), ())),
                preferred_element_type=f32,
            )
            prod = jnp.ones((ROWS, PIX), f32)
            ahead = jnp.zeros((ROWS, PIX), f32)
            for i in range(steps):
                alpha = jnp.exp(power[i * ROWS : i * ROWS + ROWS])
                gc = shade[i * ROWS : i * ROWS + ROWS]
                weight = prod * alpha
                ahead = ahead + weight * gc
                prod = prod - weight
                alpha_s[name, i] = alpha
                gc_s[name, i] = gc
            gain_s[name] = prod
            offset_s[name] = ahead
        return carry

    lax.fori_loop(0, rounds, local_pass, 0)

    def scan_pass(t, carry):
        trans = jnp.ones((1, PIX), f32)
        gains, offsets = [], []
        for b in range(blocks):
            name = t * blocks + b
            alive = b < count_ref[t]
            gains.append(jnp.where(alive, gain_s[name], 1.0))
            offsets.append(jnp.where(alive, offset_s[name], 0.0))
        for b in range(blocks):
            before, whole = scan_before(gains[b], row)
            gain_s[t * blocks + b] = before * trans
            trans = trans * whole
        incoming = jnp.zeros((1, PIX), f32)
        for b in reversed(range(blocks)):
            behind, incoming = scan_behind(gains[b], offsets[b], row, incoming)
            offset_s[t * blocks + b] = behind
        return carry

    lax.fori_loop(0, tiles, scan_pass, 0, unroll=2)

    def grad_pass(k, carry):
        for w in range(WIDE):
            name = live[k * WIDE + w]
            t, b = name // blocks, name % blocks
            prod = gain_s[name]
            weights = []
            for i in range(steps):
                weight = prod * alpha_s[name, i]
                prod = prod - weight
                weights.append(weight)
            behind = offset_s[name]
            hits = []
            for i in reversed(range(steps)):
                diff = gc_s[name, i] - behind
                hits.append(weights[i] * diff)
                behind = behind + alpha_s[name, i] * diff
            w2 = split_stack(weights)
            h2 = split_stack(hits[::-1])
            head = features[name, 18:21]
            tail = features[name, 24:27]
            colour = jnp.concatenate(
                [
                    jnp.concatenate([head, tail, jnp.zeros((2, BLOCK), f32)], axis=0),
                    jnp.concatenate([head, jnp.zeros((5, BLOCK), f32)], axis=0),
                ],
                axis=1,
            ).astype(bf16)
            image_s[t] += jnp.dot(colour, w2, preferred_element_type=f32)
            got = lax.dot_general(
                up_rows[t].astype(bf16), w2, (((1,), (1,)), ((), ())), preferred_element_type=f32
            )
            colour_grads[t, :, b, :] = got[0:3, :BLOCK] + got[0:3, BLOCK:] + got[3:6, :BLOCK]
            got = lax.dot_general(
                monomials, h2, (((1,), (1,)), ((), ())), preferred_element_type=f32
            )
            moments[t, :, b, :] = got[:, :BLOCK] + got[:, BLOCK:]
        return carry

    lax.fori_loop(0, rounds, grad_pass, 0)

    def finish(t, carry):
        image_ref[t] = image_s[t, 0:3] + image_s[t, 3:6]
        alive = block_row < count_ref[t]
        sum_h, sum_x, sum_y, sum_xx, sum_xy, sum_yy = [
            jnp.where(alive, moments[t, m], 0.0) for m in range(6)
        ]
        mid_u, mid_v = middle(t)
        off_u = mid_u - slots_ref[t, 0]
        off_v = mid_v - slots_ref[t, 1]
        con_a, con_b, con_c = (slots_ref[t, 2], slots_ref[t, 3], slots_ref[t, 4])
        sum_u = sum_x + off_u * sum_h
        sum_v = sum_y + off_v * sum_h
        grads_ref[t, 0] = con_a * sum_u + con_b * sum_v
        grads_ref[t, 1] = con_b * sum_u + con_c * sum_v
        grads_ref[t, 2] = -0.5 * (sum_xx + off_u * (sum_x + sum_u))
        grads_ref[t, 3] = -(sum_xy + off_v * sum_x + off_u * sum_v)
        grads_ref[t, 4] = -0.5 * (sum_yy + off_v * (sum_y + sum_v))
        grads_ref[t, 5] = sum_h
        for c in range(3):
            grads_ref[t, 6 + c] = jnp.where(alive, colour_grads[t, c], 0.0)
        return carry

    lax.fori_loop(0, tiles, finish, 0, unroll=2)
    gather_all(back_ref, grads_ref, sent_ref, table, table_low, 0)


def params(**kw):
    return pltpu.CompilerParams(vmem_limit_bytes=vmem_bytes, **kw)


def local(gauss_params, wanted, depth_order, block_count, image_grad):
    peers = wanted.shape[1]
    capacity = wanted.shape[2]
    tiles_here, slots = depth_order.shape
    gauss_here = gauss_params.shape[1]
    lines = capacity // LANES
    groups = gauss_here // (ROWS * LANES)
    blocks = slots // BLOCK
    shape = (groups, CHAN, ROWS, LANES)
    index_shape = (groups, ROWS, LANES)
    tables = [
        pltpu.VMEM(((CHAN - LANED) * 64, 512), bf16),
        pltpu.VMEM((FINE * 64, 256), bf16),
    ]

    def exchange(value):
        if lines != ROWS:
            value = value.transpose(0, 2, 1, 3).reshape(peers, lines, CHAN, LANES).transpose(0, 2, 1, 3)
        value = lax.all_to_all(value, "tile", split_axis=0, concat_axis=0, tiled=True)
        if lines != ROWS:
            value = value.transpose(0, 2, 1, 3).reshape(groups, ROWS, CHAN, LANES).transpose(0, 2, 1, 3)
        return value

    def invert(index):
        return pl.pallas_call(
            invert_kernel,
            out_shape=jax.ShapeDtypeStruct(index_shape, jnp.int32),
            compiler_params=params(),
        )(index)

    def gather(index, value, fine):
        return pl.pallas_call(
            lambda *refs: gather_kernel(fine, *refs),
            out_shape=jax.ShapeDtypeStruct(shape, f32),
            scratch_shapes=tables,
            compiler_params=params(),
        )(index, value)

    asked = lax.all_to_all(
        wanted.reshape(peers, lines, LANES), "tile", split_axis=0, concat_axis=0, tiled=True
    ).reshape(index_shape)
    projected = pl.pallas_call(
        project_kernel,
        out_shape=jax.ShapeDtypeStruct(shape, f32),
        scratch_shapes=[pltpu.VMEM((PARAMS, ROWS, LANES), f32)],
        compiler_params=params(),
    )(gauss_params)
    order = (
        depth_order.reshape(tiles_here, blocks, ROWS, BLOCK // ROWS)
        .transpose(0, 1, 3, 2)
        .reshape(tiles_here, blocks, BLOCK)
    )
    order_back = invert(order)
    outgoing = gather(asked, projected, FINE)
    arrived = exchange(outgoing)
    asked_back = invert(asked)
    first_tile = (lax.axis_index("tile") * tiles_here).reshape(1).astype(jnp.int32)
    steps = BLOCK // ROWS
    spare = tiles_here * blocks
    image, sent = pl.pallas_call(
        blend_kernel,
        in_specs=[
            pl.BlockSpec(memory_space=pltpu.SMEM),
            pl.BlockSpec(memory_space=pltpu.SMEM),
            pl.BlockSpec(memory_space=pltpu.VMEM),
            pl.BlockSpec(memory_space=pltpu.VMEM),
            pl.BlockSpec(memory_space=pltpu.VMEM),
            pl.BlockSpec(memory_space=pltpu.VMEM),
        ],
        out_shape=[
            jax.ShapeDtypeStruct((tiles_here, 3, PIX), f32),
            jax.ShapeDtypeStruct(shape, f32),
        ],
        scratch_shapes=tables
        + [
            pltpu.VMEM((tiles_here, CHAN, blocks, BLOCK), f32),
            pltpu.VMEM((tiles_here, CHAN, blocks, BLOCK), f32),
            pltpu.SMEM((spare + WIDE,), jnp.int32),
            pltpu.VMEM((spare + 1, 32, BLOCK), f32),
            pltpu.VMEM((tiles_here + 1, 32, PIX), f32),
            pltpu.VMEM((tiles_here + 1, ROWS, PIX), f32),
            pltpu.VMEM((spare + 1, steps, ROWS, PIX), f32),
            pltpu.VMEM((spare + 1, steps, ROWS, PIX), f32),
            pltpu.VMEM((spare + 1, ROWS, PIX), f32),
            pltpu.VMEM((spare + 1, ROWS, PIX), f32),
            pltpu.VMEM((tiles_here + 1, ROWS, PIX), f32),
            pltpu.VMEM((tiles_here + 1, ROWS, blocks, BLOCK), f32),
            pltpu.VMEM((tiles_here + 1, 3, blocks, BLOCK), f32),
        ],
        compiler_params=params(),
    )(block_count, first_tile, order, order_back, arrived, image_grad)
    returned = exchange(sent)
    param_grads = pl.pallas_call(
        return_kernel,
        out_shape=jax.ShapeDtypeStruct(gauss_params.shape, f32),
        scratch_shapes=tables
        + [
            pltpu.VMEM(shape, f32),
            pltpu.VMEM((PARAMS, ROWS, LANES), f32),
            pltpu.VMEM((PARAMS, ROWS, LANES), f32),
        ],
        compiler_params=params(),
    )(asked_back, returned, gauss_params)
    return (image, param_grads)


def solution(mesh):
    placed = (
        P(None, ("groups", "tile")),
        P(("groups", "tile"), None, None),
        P(("groups", "tile"), None),
        P(("groups", "tile")),
        P(("groups", "tile"), None, None),
    )
    return jax.shard_map(
        local,
        mesh=mesh,
        in_specs=placed,
        out_specs=(P(("groups", "tile"), None, None), P(None, ("groups", "tile"))),
        check_vma=False,
    )
```

```python
import jax
import jax.numpy as jnp
from jax import lax
from jax.experimental import pallas as pl
from jax.experimental.pallas import tpu as pltpu
from jax.sharding import PartitionSpec as P

BLOCK = 128
PIX = 256
LANES = 128
ROWS = 8
CHAN = 9
PARAMS = 14
LANED = 3
AT_ONCE = 8
AT_ONCE_BACK = 4
FINE = 2
LOCAL_WIDE = 16
GRAD_WIDE = 8

focal = 1000.0
center_u = 512.0
center_v = 512.0
dilate = 0.3
tile_row = 64
log_floor = -200.0
vmem_bytes = 56 * 1024 * 1024

f32 = jnp.float32
bf16 = jnp.bfloat16


def pieces(value, count):
    out = []
    for _ in range(count - 1):
        head = value.astype(bf16)
        out.append(head)
        value = value - head.astype(f32)
    out.append(value.astype(bf16))
    return out


def fill_table(read, table, table_low, fine):
    for c in range(CHAN - LANED):
        wide = jnp.concatenate([read(LANED + c, 0), read(LANED + c, 1)], axis=1)
        part = pieces(wide, 3 if c < fine else 2)
        rows = pl.ds(c * 64, 64)
        table[rows, 0:256] = part[0]
        table[rows, 256:512] = part[1]
        if c < fine:
            table_low[rows, :] = part[2]


def pick(index, table, table_low, fine):
    column = (index & 127) | ((index >> 13) << 7)
    row = (index >> 7) & 63
    places = lax.broadcasted_iota(jnp.int32, (256, 256), 0).astype(f32).astype(bf16)
    column = jnp.broadcast_to(column.astype(f32).astype(bf16), (256, 256))
    chosen = jnp.where(column == places, bf16(1), bf16(0))
    row_hit = jnp.broadcast_to(row, (64, 256)) == lax.broadcasted_iota(jnp.int32, (64, 256), 0)
    both = jnp.dot(
        table[...], jnp.concatenate([chosen, chosen], axis=0), preferred_element_type=f32
    )
    if fine:
        low = jnp.dot(table_low[...], chosen, preferred_element_type=f32)
    out = []
    for c in range(CHAN - LANED):
        mine = both[c * 64 : c * 64 + 64]
        if c < fine:
            mine = mine + low[c * 64 : c * 64 + 64]
        out.append(jnp.sum(jnp.where(row_hit, mine, 0.0), axis=0, keepdims=True))
    return out


def gather_all(index_ref, in_ref, out_ref, table, table_low, fine, beside=None, at_once=AT_ONCE):
    groups = in_ref.shape[0]
    quarter = groups // (ROWS // 2)
    fill_table(lambda c, half: read_half(in_ref, c, half), table, table_low, fine)

    def one(t):
        whole = index_ref[t]
        row, column = whole >> 7, whole & 127
        found = [jnp.zeros((ROWS, LANES), f32) for _ in range(LANED)]
        for half in range(ROWS // 2):
            for q in range(half * quarter, half * quarter + quarter):
                for s in range(ROWS):
                    hit = row == q * ROWS + s
                    for c in range(LANED):
                        line = jnp.broadcast_to(in_ref[q, c, s : s + 1, :], (ROWS, LANES))
                        found[c] = jnp.where(
                            hit, jnp.take_along_axis(line, column, axis=1), found[c]
                        )
            index = jnp.concatenate(
                [index_ref[t, 2 * half : 2 * half + 1, :], index_ref[t, 2 * half + 1 : 2 * half + 2, :]],
                axis=1,
            )
            for c, line in enumerate(pick(index, table, table_low, fine)):
                out_ref[t, LANED + c, 2 * half : 2 * half + 1, :] = line[:, :LANES]
                out_ref[t, LANED + c, 2 * half + 1 : 2 * half + 2, :] = line[:, LANES:]
        for c in range(LANED):
            out_ref[t, c] = found[c]

    def step(k, carry):
        for u in range(at_once):
            if beside is not None:
                beside(jnp.maximum(k - 1, 0) * at_once + u)
        for u in range(at_once):
            one(k * at_once + u)
        return carry

    if beside is not None:
        for u in range(at_once):
            out_ref[u] = jnp.zeros_like(out_ref[u])
    lax.fori_loop(0, groups // at_once, step, 0)
    if beside is not None:
        for u in range(at_once):
            beside(groups - at_once + u)


def invert_kernel(index_ref, out_ref):
    place = lax.broadcasted_iota(jnp.int32, (LANES, LANES), 0)
    lane = lax.broadcasted_iota(jnp.int32, (LANES, LANES), 1).astype(f32)

    def step(t, total):
        for s in range(ROWS):
            line = index_ref[t, s : s + 1, :]
            row_hit = jnp.broadcast_to(line >> 7, (LANES, LANES)) == place
            column_hit = jnp.broadcast_to(line & 127, (LANES, LANES)) == place
            here = (t * ROWS + s).astype(f32)
            left = jnp.concatenate(
                [jnp.where(row_hit, here, 0.0).astype(bf16), jnp.where(row_hit, lane, 0.0).astype(bf16)],
                axis=0,
            )
            right = jnp.where(column_hit, 1.0, 0.0).astype(bf16)
            total = total + lax.dot_general(
                left, right, (((1,), (1,)), ((), ())), preferred_element_type=f32
            )
        return total

    total = lax.fori_loop(0, index_ref.shape[0], step, jnp.zeros((2 * LANES, LANES), f32))
    value = (total[:LANES] * float(LANES) + total[LANES:]).astype(jnp.int32)
    for t in range(index_ref.shape[0]):
        out_ref[t] = value[t * ROWS : t * ROWS + ROWS]


def project_core(raw):
    pos_x, pos_y, depth = (raw[0], raw[1], raw[2])
    scale_x, scale_y, scale_z = (jnp.exp(raw[3]), jnp.exp(raw[4]), jnp.exp(raw[5]))
    norm_inv = 1.0 / jnp.sqrt(raw[6] * raw[6] + raw[7] * raw[7] + raw[8] * raw[8] + raw[9] * raw[9])
    q_real, q_one, q_two, q_three = (
        raw[6] * norm_inv,
        raw[7] * norm_inv,
        raw[8] * norm_inv,
        raw[9] * norm_inv,
    )
    rot = [
        [
            1.0 - 2.0 * (q_two * q_two + q_three * q_three),
            2.0 * (q_one * q_two - q_real * q_three),
            2.0 * (q_one * q_three + q_real * q_two),
        ],
        [
            2.0 * (q_one * q_two + q_real * q_three),
            1.0 - 2.0 * (q_one * q_one + q_three * q_three),
            2.0 * (q_two * q_three - q_real * q_one),
        ],
        [
            2.0 * (q_one * q_three - q_real * q_two),
            2.0 * (q_two * q_three + q_real * q_one),
            1.0 - 2.0 * (q_one * q_one + q_two * q_two),
        ],
    ]
    scales = [scale_x, scale_y, scale_z]
    mixed = [[rot[i][k] * scales[k] for k in range(3)] for i in range(3)]
    cov = [
        [
            mixed[i][0] * mixed[j][0] + mixed[i][1] * mixed[j][1] + mixed[i][2] * mixed[j][2]
            for j in range(3)
        ]
        for i in range(3)
    ]
    depth_inv = 1.0 / depth
    jac_uu = focal * depth_inv
    jac_uz = -jac_uu * (pos_x * depth_inv)
    jac_vv = jac_uu
    jac_vz = -jac_uu * (pos_y * depth_inv)
    upper = [jac_uu * cov[0][k] + jac_uz * cov[2][k] for k in range(3)]
    lower = [jac_vv * cov[1][k] + jac_vz * cov[2][k] for k in range(3)]
    first = upper[0] * jac_uu + upper[2] * jac_uz + dilate
    cross = upper[1] * jac_vv + upper[2] * jac_vz
    second = lower[1] * jac_vv + lower[2] * jac_vz + dilate
    det_inv = 1.0 / (first * second - cross * cross)
    return [
        focal * pos_x * depth_inv + center_u,
        focal * pos_y * depth_inv + center_v,
        second * det_inv,
        -cross * det_inv,
        first * det_inv,
    ]


def sigmoid(x):
    return 1.0 / (1.0 + jnp.exp(-x))


def project_kernel(params_ref, out_ref, raw):
    def step(t, carry):
        for s in range(ROWS):
            raw[:, s, :] = params_ref[:, pl.ds(pl.multiple_of((t * ROWS + s) * LANES, LANES), LANES)]
        rows = project_core([raw[k] for k in range(10)])
        for c in range(5):
            out_ref[t, c] = rows[c]
        out_ref[t, 5] = sigmoid(raw[10])
        for c in range(3):
            out_ref[t, 6 + c] = raw[11 + c]
        return carry

    lax.fori_loop(0, out_ref.shape[0], step, 0)


def read_half(ref, c, half):
    groups = ref.shape[0] // 2
    return jnp.concatenate([ref[half * groups + q, c] for q in range(groups)], axis=0)


def gather_kernel(fine, index_ref, in_ref, out_ref, table, table_low):
    gather_all(index_ref, in_ref, out_ref, table, table_low, fine)


def return_kernel(index_ref, grads_ref, params_ref, out_ref, table, table_low, summed, raw, stage):
    def back(t):
        for s in range(ROWS):
            raw[:, s, :] = params_ref[:, pl.ds(pl.multiple_of((t * ROWS + s) * LANES, LANES), LANES)]
        _, pull = jax.vjp(project_core, [raw[k] for k in range(10)])
        core = pull([summed[t, c] for c in range(5)])[0]
        for k in range(10):
            stage[k] = core[k]
        stage[10] = summed[t, 5] * sigmoid(-raw[10])
        for c in range(3):
            stage[11 + c] = summed[t, 6 + c]
        for s in range(ROWS):
            out_ref[:, pl.ds(pl.multiple_of((t * ROWS + s) * LANES, LANES), LANES)] = stage[:, s, :]

    gather_all(index_ref, grads_ref, summed, table, table_low, 0, back, AT_ONCE_BACK)


def scan_before(value, row):
    total = value
    for shift in (1, 2, 4):
        total = total * jnp.where(row >= shift, pltpu.roll(total, shift, 0), 1.0)
    before = jnp.where(row >= 1, pltpu.roll(total, 1, 0), 1.0)
    return before, total[ROWS - 1 : ROWS, :]


def scan_behind(gain, offset, row, incoming):
    for shift in (1, 2, 4):
        inside = row < ROWS - shift
        offset = offset + gain * jnp.where(inside, pltpu.roll(offset, ROWS - shift, 0), 0.0)
        gain = gain * jnp.where(inside, pltpu.roll(gain, ROWS - shift, 0), 1.0)
    value = offset + gain * incoming
    behind = jnp.where(row < ROWS - 1, pltpu.roll(value, ROWS - 1, 0), incoming)
    return behind, value[0:1, :]


def two_rows(value):
    head = value.astype(bf16)
    return head, (value - head.astype(f32)).astype(bf16)


def split_stack(values):
    both = [two_rows(value) for value in values]
    return jnp.concatenate([head for head, _ in both] + [tail for _, tail in both], axis=0)


def blend_kernel(
    count_ref,
    first_ref,
    order_ref,
    back_ref,
    arrived_ref,
    upstream_ref,
    image_ref,
    sent_ref,
    table,
    table_low,
    slots_ref,
    grads_ref,
    live,
    features,
    basis,
    up_rows,
    alpha_s,
    gc_s,
    gain_s,
    offset_s,
    image_s,
    moments,
    colour_grads,
):
    gather_all(order_ref, arrived_ref, slots_ref, table, table_low, FINE)
    tiles, _, blocks, _ = slots_ref.shape
    steps = BLOCK // ROWS
    spare = tiles * blocks
    pixel = lax.broadcasted_iota(jnp.int32, (1, PIX), 1)
    x = (pixel & 15).astype(f32) - 7.5
    y = (pixel >> 4).astype(f32) - 7.5
    row = lax.broadcasted_iota(jnp.int32, (ROWS, PIX), 0)
    block_row = lax.broadcasted_iota(jnp.int32, (blocks, BLOCK), 0)
    six = jnp.concatenate([jnp.ones_like(x), x, y, x * x, x * y, y * y], axis=0)
    power_basis = jnp.concatenate([six, six, six, jnp.zeros((14, PIX), f32)], axis=0).astype(bf16)
    monomials = jnp.concatenate([six, jnp.zeros((2, PIX), f32)], axis=0).astype(bf16)

    def middle(t):
        tile = first_ref[0] + t
        return (
            ((tile % tile_row) * 16 + 8).astype(f32),
            ((tile // tile_row) * 16 + 8).astype(f32),
        )

    basis[...] = jnp.zeros_like(basis)
    features[pl.ds(spare, 1)] = jnp.zeros((1, 32, BLOCK), f32)
    features[:, 27:32, :] = jnp.zeros((spare + 1, 5, BLOCK), f32)
    up_rows[pl.ds(tiles, 1)] = jnp.zeros((1, ROWS, PIX), f32)
    image_s[...] = jnp.zeros_like(image_s)

    def prepare(t, total):
        up = upstream_ref[t]
        up_head = up.astype(bf16).astype(f32)
        up_tail = up - up_head
        basis[t, 18:21, :] = up_head
        basis[t, 21:24, :] = up_tail
        basis[t, 24:27, :] = up_head
        up_rows[t] = jnp.concatenate([up_head, up_tail, jnp.zeros((2, PIX), f32)], axis=0)
        mid_u, mid_v = middle(t)
        off_u = mid_u - slots_ref[t, 0]
        off_v = mid_v - slots_ref[t, 1]
        con_a, con_b, con_c = (slots_ref[t, 2], slots_ref[t, 3], slots_ref[t, 4])
        log_op = jnp.maximum(jnp.log(slots_ref[t, 5]), log_floor)
        side_u = con_a * off_u + con_b * off_v
        side_v = con_b * off_u + con_c * off_v
        coefs = [
            log_op - 0.5 * (off_u * side_u + off_v * side_v),
            -side_u,
            -side_v,
            -0.5 * con_a,
            -con_b,
            -0.5 * con_c,
        ]
        here = pl.ds(t * blocks, blocks)
        for m, coef in enumerate(coefs):
            for k, part in enumerate(pieces(coef, 3)):
                features[here, 6 * k + m, :] = part.astype(f32)
        for c in range(3):
            head, tail = two_rows(slots_ref[t, 6 + c])
            features[here, 18 + c, :] = head.astype(f32)
            features[here, 21 + c, :] = head.astype(f32)
            features[here, 24 + c, :] = tail.astype(f32)
        for b in range(blocks):
            live[total] = t * blocks + b
            total = total + (b < count_ref[t]).astype(jnp.int32)
        return total

    total = lax.fori_loop(0, tiles, prepare, jnp.int32(0), unroll=4)
    for k in range(LOCAL_WIDE):
        live[total + k] = spare

    def local_pass(k, carry):
        for w in range(LOCAL_WIDE):
            name = live[k * LOCAL_WIDE + w]
            block = features[name].astype(bf16)
            power = lax.dot_general(
                block, power_basis, (((0,), (0,)), ((), ())), preferred_element_type=f32
            )
            shade = lax.dot_general(
                block,
                basis[name // blocks].astype(bf16),
                (((0,), (0,)), ((), ())),
                preferred_element_type=f32,
            )
            prod = jnp.ones((ROWS, PIX), f32)
            ahead = jnp.zeros((ROWS, PIX), f32)
            for i in range(steps):
                alpha = jnp.exp(power[i * ROWS : i * ROWS + ROWS])
                gc = shade[i * ROWS : i * ROWS + ROWS]
                weight = prod * alpha
                ahead = ahead + weight * gc
                prod = prod - weight
                alpha_s[name, i] = alpha
                gc_s[name, i] = gc
            gain_s[name] = prod
            offset_s[name] = ahead
        return carry

    lax.fori_loop(0, (total + LOCAL_WIDE - 1) // LOCAL_WIDE, local_pass, 0)

    def scan_pass(t, carry):
        trans = jnp.ones((1, PIX), f32)
        gains, offsets = [], []
        for b in range(blocks):
            name = t * blocks + b
            alive = b < count_ref[t]
            gains.append(jnp.where(alive, gain_s[name], 1.0))
            offsets.append(jnp.where(alive, offset_s[name], 0.0))
        for b in range(blocks):
            before, whole = scan_before(gains[b], row)
            gain_s[t * blocks + b] = before * trans
            trans = trans * whole
        incoming = jnp.zeros((1, PIX), f32)
        for b in reversed(range(blocks)):
            behind, incoming = scan_behind(gains[b], offsets[b], row, incoming)
            offset_s[t * blocks + b] = behind
        return carry

    lax.fori_loop(0, tiles, scan_pass, 0, unroll=4)

    def grad_pass(k, carry):
        for w in range(GRAD_WIDE):
            name = live[k * GRAD_WIDE + w]
            t, b = name // blocks, name % blocks
            prod = gain_s[name]
            weights = []
            for i in range(steps):
                weight = prod * alpha_s[name, i]
                prod = prod - weight
                weights.append(weight)
            behind = offset_s[name]
            hits = []
            for i in reversed(range(steps)):
                diff = gc_s[name, i] - behind
                hits.append(weights[i] * diff)
                behind = behind + alpha_s[name, i] * diff
            w2 = split_stack(weights)
            h2 = split_stack(hits[::-1])
            head = features[name, 18:21]
            tail = features[name, 24:27]
            colour = jnp.concatenate(
                [
                    jnp.concatenate([head, tail, jnp.zeros((2, BLOCK), f32)], axis=0),
                    jnp.concatenate([head, jnp.zeros((5, BLOCK), f32)], axis=0),
                ],
                axis=1,
            ).astype(bf16)
            image_s[t] += jnp.dot(colour, w2, preferred_element_type=f32)
            got = lax.dot_general(
                up_rows[t].astype(bf16), w2, (((1,), (1,)), ((), ())), preferred_element_type=f32
            )
            colour_grads[t, :, b, :] = got[0:3, :BLOCK] + got[0:3, BLOCK:] + got[3:6, :BLOCK]
            got = lax.dot_general(
                monomials, h2, (((1,), (1,)), ((), ())), preferred_element_type=f32
            )
            moments[t, :, b, :] = got[:, :BLOCK] + got[:, BLOCK:]
        return carry

    lax.fori_loop(0, (total + GRAD_WIDE - 1) // GRAD_WIDE, grad_pass, 0)

    def finish(t, carry):
        image_ref[t] = image_s[t, 0:3] + image_s[t, 3:6]
        alive = block_row < count_ref[t]
        sum_h, sum_x, sum_y, sum_xx, sum_xy, sum_yy = [
            jnp.where(alive, moments[t, m], 0.0) for m in range(6)
        ]
        mid_u, mid_v = middle(t)
        off_u = mid_u - slots_ref[t, 0]
        off_v = mid_v - slots_ref[t, 1]
        con_a, con_b, con_c = (slots_ref[t, 2], slots_ref[t, 3], slots_ref[t, 4])
        sum_u = sum_x + off_u * sum_h
        sum_v = sum_y + off_v * sum_h
        grads_ref[t, 0] = con_a * sum_u + con_b * sum_v
        grads_ref[t, 1] = con_b * sum_u + con_c * sum_v
        grads_ref[t, 2] = -0.5 * (sum_xx + off_u * (sum_x + sum_u))
        grads_ref[t, 3] = -(sum_xy + off_v * sum_x + off_u * sum_v)
        grads_ref[t, 4] = -0.5 * (sum_yy + off_v * (sum_y + sum_v))
        grads_ref[t, 5] = sum_h
        for c in range(3):
            grads_ref[t, 6 + c] = jnp.where(alive, colour_grads[t, c], 0.0)
        return carry

    lax.fori_loop(0, tiles, finish, 0, unroll=4)
    gather_all(back_ref, grads_ref, sent_ref, table, table_low, 0)


def params(**kw):
    return pltpu.CompilerParams(vmem_limit_bytes=vmem_bytes, **kw)


def local(gauss_params, wanted, depth_order, block_count, image_grad):
    peers = wanted.shape[1]
    capacity = wanted.shape[2]
    tiles_here, slots = depth_order.shape
    gauss_here = gauss_params.shape[1]
    lines = capacity // LANES
    groups = gauss_here // (ROWS * LANES)
    blocks = slots // BLOCK
    shape = (groups, CHAN, ROWS, LANES)
    index_shape = (groups, ROWS, LANES)
    tables = [
        pltpu.VMEM(((CHAN - LANED) * 64, 512), bf16),
        pltpu.VMEM((FINE * 64, 256), bf16),
    ]

    def exchange(value):
        if lines != ROWS:
            value = value.transpose(0, 2, 1, 3).reshape(peers, lines, CHAN, LANES).transpose(0, 2, 1, 3)
        value = lax.all_to_all(value, "tile", split_axis=0, concat_axis=0, tiled=True)
        if lines != ROWS:
            value = value.transpose(0, 2, 1, 3).reshape(groups, ROWS, CHAN, LANES).transpose(0, 2, 1, 3)
        return value

    def invert(index):
        return pl.pallas_call(
            invert_kernel,
            out_shape=jax.ShapeDtypeStruct(index_shape, jnp.int32),
            compiler_params=params(),
        )(index)

    def gather(index, value, fine):
        return pl.pallas_call(
            lambda *refs: gather_kernel(fine, *refs),
            out_shape=jax.ShapeDtypeStruct(shape, f32),
            scratch_shapes=tables,
            compiler_params=params(),
        )(index, value)

    asked = lax.all_to_all(
        wanted.reshape(peers, lines, LANES), "tile", split_axis=0, concat_axis=0, tiled=True
    ).reshape(index_shape)
    projected = pl.pallas_call(
        project_kernel,
        out_shape=jax.ShapeDtypeStruct(shape, f32),
        scratch_shapes=[pltpu.VMEM((PARAMS, ROWS, LANES), f32)],
        compiler_params=params(),
    )(gauss_params)
    order = (
        depth_order.reshape(tiles_here, blocks, ROWS, BLOCK // ROWS)
        .transpose(0, 1, 3, 2)
        .reshape(tiles_here, blocks, BLOCK)
    )
    order_back = invert(order)
    outgoing = gather(asked, projected, FINE)
    arrived = exchange(outgoing)
    asked_back = invert(asked)
    first_tile = (lax.axis_index("tile") * tiles_here).reshape(1).astype(jnp.int32)
    steps = BLOCK // ROWS
    spare = tiles_here * blocks
    image, sent = pl.pallas_call(
        blend_kernel,
        in_specs=[
            pl.BlockSpec(memory_space=pltpu.SMEM),
            pl.BlockSpec(memory_space=pltpu.SMEM),
            pl.BlockSpec(memory_space=pltpu.VMEM),
            pl.BlockSpec(memory_space=pltpu.VMEM),
            pl.BlockSpec(memory_space=pltpu.VMEM),
            pl.BlockSpec(memory_space=pltpu.VMEM),
        ],
        out_shape=[
            jax.ShapeDtypeStruct((tiles_here, 3, PIX), f32),
            jax.ShapeDtypeStruct(shape, f32),
        ],
        scratch_shapes=tables
        + [
            pltpu.VMEM((tiles_here, CHAN, blocks, BLOCK), f32),
            pltpu.VMEM((tiles_here, CHAN, blocks, BLOCK), f32),
            pltpu.SMEM((spare + LOCAL_WIDE,), jnp.int32),
            pltpu.VMEM((spare + 1, 32, BLOCK), f32),
            pltpu.VMEM((tiles_here + 1, 32, PIX), f32),
            pltpu.VMEM((tiles_here + 1, ROWS, PIX), f32),
            pltpu.VMEM((spare + 1, steps, ROWS, PIX), f32),
            pltpu.VMEM((spare + 1, steps, ROWS, PIX), f32),
            pltpu.VMEM((spare + 1, ROWS, PIX), f32),
            pltpu.VMEM((spare + 1, ROWS, PIX), f32),
            pltpu.VMEM((tiles_here + 1, ROWS, PIX), f32),
            pltpu.VMEM((tiles_here + 1, ROWS, blocks, BLOCK), f32),
            pltpu.VMEM((tiles_here + 1, 3, blocks, BLOCK), f32),
        ],
        compiler_params=params(),
    )(block_count, first_tile, order, order_back, arrived, image_grad)
    returned = exchange(sent)
    param_grads = pl.pallas_call(
        return_kernel,
        out_shape=jax.ShapeDtypeStruct(gauss_params.shape, f32),
        scratch_shapes=tables
        + [
            pltpu.VMEM(shape, f32),
            pltpu.VMEM((PARAMS, ROWS, LANES), f32),
            pltpu.VMEM((PARAMS, ROWS, LANES), f32),
        ],
        compiler_params=params(),
    )(asked_back, returned, gauss_params)
    return (image, param_grads)


def solution(mesh):
    placed = (
        P(None, ("groups", "tile")),
        P(("groups", "tile"), None, None),
        P(("groups", "tile"), None),
        P(("groups", "tile")),
        P(("groups", "tile"), None, None),
    )
    return jax.shard_map(
        local,
        mesh=mesh,
        in_specs=placed,
        out_specs=(P(("groups", "tile"), None, None), P(None, ("groups", "tile"))),
        check_vma=False,
    )
```

```python
import jax
import jax.numpy as jnp
from jax import lax
from jax.experimental import pallas as pl
from jax.experimental.pallas import tpu as pltpu
from jax.sharding import PartitionSpec as P

BLOCK = 128
PIX = 256
LANES = 128
ROWS = 8
CHAN = 9
PARAMS = 14
LANED = 3
AT_ONCE = 8
AT_ONCE_BACK = 4
FINE = 2
LOCAL_WIDE = 16
GRAD_WIDE = 8

focal = 1000.0
center_u = 512.0
center_v = 512.0
dilate = 0.3
tile_row = 64
log_floor = -200.0
vmem_bytes = 56 * 1024 * 1024

f32 = jnp.float32
bf16 = jnp.bfloat16


def pieces(value, count):
    out = []
    for _ in range(count - 1):
        head = value.astype(bf16)
        out.append(head)
        value = value - head.astype(f32)
    out.append(value.astype(bf16))
    return out


def fill_table(read, table, table_low, fine):
    for c in range(CHAN - LANED):
        wide = jnp.concatenate([read(LANED + c, 0), read(LANED + c, 1)], axis=1)
        part = pieces(wide, 3 if c < fine else 2)
        rows = pl.ds(c * 64, 64)
        table[rows, 0:256] = part[0]
        table[rows, 256:512] = part[1]
        if c < fine:
            table_low[rows, :] = part[2]


def pick(index, table, table_low, fine):
    column = (index & 127) | ((index >> 13) << 7)
    row = (index >> 7) & 63
    places = lax.broadcasted_iota(jnp.int32, (256, 256), 0).astype(f32).astype(bf16)
    column = jnp.broadcast_to(column.astype(f32).astype(bf16), (256, 256))
    chosen = jnp.where(column == places, bf16(1), bf16(0))
    row_hit = jnp.broadcast_to(row, (64, 256)) == lax.broadcasted_iota(jnp.int32, (64, 256), 0)
    both = jnp.dot(
        table[...], jnp.concatenate([chosen, chosen], axis=0), preferred_element_type=f32
    )
    if fine:
        low = jnp.dot(table_low[...], chosen, preferred_element_type=f32)
    out = []
    for c in range(CHAN - LANED):
        mine = both[c * 64 : c * 64 + 64]
        if c < fine:
            mine = mine + low[c * 64 : c * 64 + 64]
        out.append(jnp.sum(jnp.where(row_hit, mine, 0.0), axis=0, keepdims=True))
    return out


def gather_all(index_ref, in_ref, out_ref, table, table_low, fine, beside=None, at_once=AT_ONCE, filled=False):
    groups = in_ref.shape[0]
    quarter = groups // (ROWS // 2)
    if not filled:
        fill_table(lambda c, half: read_half(in_ref, c, half), table, table_low, fine)

    def one(t):
        whole = index_ref[t]
        row, column = whole >> 7, whole & 127
        found = [jnp.zeros((ROWS, LANES), f32) for _ in range(LANED)]
        for half in range(ROWS // 2):
            for q in range(half * quarter, half * quarter + quarter):
                for s in range(ROWS):
                    hit = row == q * ROWS + s
                    for c in range(LANED):
                        line = jnp.broadcast_to(in_ref[q, c, s : s + 1, :], (ROWS, LANES))
                        found[c] = jnp.where(
                            hit, jnp.take_along_axis(line, column, axis=1), found[c]
                        )
            index = jnp.concatenate(
                [index_ref[t, 2 * half : 2 * half + 1, :], index_ref[t, 2 * half + 1 : 2 * half + 2, :]],
                axis=1,
            )
            for c, line in enumerate(pick(index, table, table_low, fine)):
                out_ref[t, LANED + c, 2 * half : 2 * half + 1, :] = line[:, :LANES]
                out_ref[t, LANED + c, 2 * half + 1 : 2 * half + 2, :] = line[:, LANES:]
        for c in range(LANED):
            out_ref[t, c] = found[c]

    def step(k, carry):
        for u in range(at_once):
            if beside is not None:
                beside(jnp.maximum(k - 1, 0) * at_once + u)
        for u in range(at_once):
            one(k * at_once + u)
        return carry

    if beside is not None:
        for u in range(at_once):
            out_ref[u] = jnp.zeros_like(out_ref[u])
    lax.fori_loop(0, groups // at_once, step, 0)
    if beside is not None:
        for u in range(at_once):
            beside(groups - at_once + u)


def invert_kernel(index_ref, out_ref):
    place = lax.broadcasted_iota(jnp.int32, (LANES, LANES), 0)
    lane = lax.broadcasted_iota(jnp.int32, (LANES, LANES), 1).astype(f32)

    def step(t, total):
        for s in range(ROWS):
            line = index_ref[t, s : s + 1, :]
            row_hit = jnp.broadcast_to(line >> 7, (LANES, LANES)) == place
            column_hit = jnp.broadcast_to(line & 127, (LANES, LANES)) == place
            here = (t * ROWS + s).astype(f32)
            left = jnp.concatenate(
                [jnp.where(row_hit, here, 0.0).astype(bf16), jnp.where(row_hit, lane, 0.0).astype(bf16)],
                axis=0,
            )
            right = jnp.where(column_hit, 1.0, 0.0).astype(bf16)
            total = total + lax.dot_general(
                left, right, (((1,), (1,)), ((), ())), preferred_element_type=f32
            )
        return total

    total = lax.fori_loop(0, index_ref.shape[0], step, jnp.zeros((2 * LANES, LANES), f32))
    value = (total[:LANES] * float(LANES) + total[LANES:]).astype(jnp.int32)
    for t in range(index_ref.shape[0]):
        out_ref[t] = value[t * ROWS : t * ROWS + ROWS]


def project_core(raw):
    pos_x, pos_y, depth = (raw[0], raw[1], raw[2])
    scale_x, scale_y, scale_z = (jnp.exp(raw[3]), jnp.exp(raw[4]), jnp.exp(raw[5]))
    norm_inv = 1.0 / jnp.sqrt(raw[6] * raw[6] + raw[7] * raw[7] + raw[8] * raw[8] + raw[9] * raw[9])
    q_real, q_one, q_two, q_three = (
        raw[6] * norm_inv,
        raw[7] * norm_inv,
        raw[8] * norm_inv,
        raw[9] * norm_inv,
    )
    rot = [
        [
            1.0 - 2.0 * (q_two * q_two + q_three * q_three),
            2.0 * (q_one * q_two - q_real * q_three),
            2.0 * (q_one * q_three + q_real * q_two),
        ],
        [
            2.0 * (q_one * q_two + q_real * q_three),
            1.0 - 2.0 * (q_one * q_one + q_three * q_three),
            2.0 * (q_two * q_three - q_real * q_one),
        ],
        [
            2.0 * (q_one * q_three - q_real * q_two),
            2.0 * (q_two * q_three + q_real * q_one),
            1.0 - 2.0 * (q_one * q_one + q_two * q_two),
        ],
    ]
    scales = [scale_x, scale_y, scale_z]
    mixed = [[rot[i][k] * scales[k] for k in range(3)] for i in range(3)]
    cov = [
        [
            mixed[i][0] * mixed[j][0] + mixed[i][1] * mixed[j][1] + mixed[i][2] * mixed[j][2]
            for j in range(3)
        ]
        for i in range(3)
    ]
    depth_inv = 1.0 / depth
    jac_uu = focal * depth_inv
    jac_uz = -jac_uu * (pos_x * depth_inv)
    jac_vv = jac_uu
    jac_vz = -jac_uu * (pos_y * depth_inv)
    upper = [jac_uu * cov[0][k] + jac_uz * cov[2][k] for k in range(3)]
    lower = [jac_vv * cov[1][k] + jac_vz * cov[2][k] for k in range(3)]
    first = upper[0] * jac_uu + upper[2] * jac_uz + dilate
    cross = upper[1] * jac_vv + upper[2] * jac_vz
    second = lower[1] * jac_vv + lower[2] * jac_vz + dilate
    det_inv = 1.0 / (first * second - cross * cross)
    return [
        focal * pos_x * depth_inv + center_u,
        focal * pos_y * depth_inv + center_v,
        second * det_inv,
        -cross * det_inv,
        first * det_inv,
    ]


def sigmoid(x):
    return 1.0 / (1.0 + jnp.exp(-x))


def project_kernel(params_ref, out_ref, table, table_low, raw):
    def step(t, carry):
        for s in range(ROWS):
            raw[:, s, :] = params_ref[:, pl.ds(pl.multiple_of((t * ROWS + s) * LANES, LANES), LANES)]
        rows = project_core([raw[k] for k in range(10)])
        for c in range(5):
            out_ref[t, c] = rows[c]
        out_ref[t, 5] = sigmoid(raw[10])
        for c in range(3):
            out_ref[t, 6 + c] = raw[11 + c]
        return carry

    lax.fori_loop(0, out_ref.shape[0], step, 0)
    fill_table(lambda c, half: read_half(out_ref, c, half), table, table_low, FINE)


def read_half(ref, c, half):
    groups = ref.shape[0] // 2
    return jnp.concatenate([ref[half * groups + q, c] for q in range(groups)], axis=0)


def gather_kernel(index_ref, in_ref, table, table_low, out_ref):
    gather_all(index_ref, in_ref, out_ref, table, table_low, FINE, filled=True)


def return_kernel(index_ref, grads_ref, params_ref, out_ref, table, table_low, summed, raw, stage):
    def back(t):
        for s in range(ROWS):
            raw[:, s, :] = params_ref[:, pl.ds(pl.multiple_of((t * ROWS + s) * LANES, LANES), LANES)]
        _, pull = jax.vjp(project_core, [raw[k] for k in range(10)])
        core = pull([summed[t, c] for c in range(5)])[0]
        for k in range(10):
            stage[k] = core[k]
        stage[10] = summed[t, 5] * sigmoid(-raw[10])
        for c in range(3):
            stage[11 + c] = summed[t, 6 + c]
        for s in range(ROWS):
            out_ref[:, pl.ds(pl.multiple_of((t * ROWS + s) * LANES, LANES), LANES)] = stage[:, s, :]

    gather_all(index_ref, grads_ref, summed, table, table_low, 0, back, AT_ONCE_BACK)


def scan_before(value, row):
    total = value
    for shift in (1, 2, 4):
        total = total * jnp.where(row >= shift, pltpu.roll(total, shift, 0), 1.0)
    before = jnp.where(row >= 1, pltpu.roll(total, 1, 0), 1.0)
    return before, total[ROWS - 1 : ROWS, :]


def scan_behind(gain, offset, row, incoming):
    for shift in (1, 2, 4):
        inside = row < ROWS - shift
        offset = offset + gain * jnp.where(inside, pltpu.roll(offset, ROWS - shift, 0), 0.0)
        gain = gain * jnp.where(inside, pltpu.roll(gain, ROWS - shift, 0), 1.0)
    value = offset + gain * incoming
    behind = jnp.where(row < ROWS - 1, pltpu.roll(value, ROWS - 1, 0), incoming)
    return behind, value[0:1, :]


def two_rows(value):
    head = value.astype(bf16)
    return head, (value - head.astype(f32)).astype(bf16)


def split_stack(values):
    both = [two_rows(value) for value in values]
    return jnp.concatenate([head for head, _ in both] + [tail for _, tail in both], axis=0)


def blend_kernel(
    count_ref,
    first_ref,
    order_ref,
    back_ref,
    arrived_ref,
    upstream_ref,
    image_ref,
    sent_ref,
    table,
    table_low,
    slots_ref,
    grads_ref,
    live,
    features,
    basis,
    up_rows,
    alpha_s,
    gc_s,
    gain_s,
    offset_s,
    image_s,
    moments,
    colour_grads,
):
    gather_all(order_ref, arrived_ref, slots_ref, table, table_low, FINE)
    tiles, _, blocks, _ = slots_ref.shape
    steps = BLOCK // ROWS
    spare = tiles * blocks
    pixel = lax.broadcasted_iota(jnp.int32, (1, PIX), 1)
    x = (pixel & 15).astype(f32) - 7.5
    y = (pixel >> 4).astype(f32) - 7.5
    row = lax.broadcasted_iota(jnp.int32, (ROWS, PIX), 0)
    block_row = lax.broadcasted_iota(jnp.int32, (blocks, BLOCK), 0)
    six = jnp.concatenate([jnp.ones_like(x), x, y, x * x, x * y, y * y], axis=0)
    power_basis = jnp.concatenate([six, six, six, jnp.zeros((14, PIX), f32)], axis=0).astype(bf16)
    monomials = jnp.concatenate([six, jnp.zeros((2, PIX), f32)], axis=0).astype(bf16)

    def middle(t):
        tile = first_ref[0] + t
        return (
            ((tile % tile_row) * 16 + 8).astype(f32),
            ((tile // tile_row) * 16 + 8).astype(f32),
        )

    basis[...] = jnp.zeros_like(basis)
    features[pl.ds(spare, 1)] = jnp.zeros((1, 32, BLOCK), f32)
    features[:, 27:32, :] = jnp.zeros((spare + 1, 5, BLOCK), f32)
    up_rows[pl.ds(tiles, 1)] = jnp.zeros((1, ROWS, PIX), f32)
    image_s[...] = jnp.zeros_like(image_s)

    def prepare(t, total):
        up = upstream_ref[t]
        up_head = up.astype(bf16).astype(f32)
        up_tail = up - up_head
        basis[t, 18:21, :] = up_head
        basis[t, 21:24, :] = up_tail
        basis[t, 24:27, :] = up_head
        up_rows[t] = jnp.concatenate([up_head, up_tail, jnp.zeros((2, PIX), f32)], axis=0)
        mid_u, mid_v = middle(t)
        off_u = mid_u - slots_ref[t, 0]
        off_v = mid_v - slots_ref[t, 1]
        con_a, con_b, con_c = (slots_ref[t, 2], slots_ref[t, 3], slots_ref[t, 4])
        log_op = jnp.maximum(jnp.log(slots_ref[t, 5]), log_floor)
        side_u = con_a * off_u + con_b * off_v
        side_v = con_b * off_u + con_c * off_v
        coefs = [
            log_op - 0.5 * (off_u * side_u + off_v * side_v),
            -side_u,
            -side_v,
            -0.5 * con_a,
            -con_b,
            -0.5 * con_c,
        ]
        here = pl.ds(t * blocks, blocks)
        for m, coef in enumerate(coefs):
            for k, part in enumerate(pieces(coef, 3)):
                features[here, 6 * k + m, :] = part.astype(f32)
        for c in range(3):
            head, tail = two_rows(slots_ref[t, 6 + c])
            features[here, 18 + c, :] = head.astype(f32)
            features[here, 21 + c, :] = head.astype(f32)
            features[here, 24 + c, :] = tail.astype(f32)
        for b in range(blocks):
            live[total] = t * blocks + b
            total = total + (b < count_ref[t]).astype(jnp.int32)
        return total

    total = lax.fori_loop(0, tiles, prepare, jnp.int32(0), unroll=4)
    for k in range(LOCAL_WIDE):
        live[total + k] = spare

    def local_pass(k, carry):
        for w in range(LOCAL_WIDE):
            name = live[k * LOCAL_WIDE + w]
            block = features[name].astype(bf16)
            power = lax.dot_general(
                block, power_basis, (((0,), (0,)), ((), ())), preferred_element_type=f32
            )
            shade = lax.dot_general(
                block,
                basis[name // blocks].astype(bf16),
                (((0,), (0,)), ((), ())),
                preferred_element_type=f32,
            )
            prod = jnp.ones((ROWS, PIX), f32)
            ahead = jnp.zeros((ROWS, PIX), f32)
            for i in range(steps):
                alpha = jnp.exp(power[i * ROWS : i * ROWS + ROWS])
                gc = shade[i * ROWS : i * ROWS + ROWS]
                weight = prod * alpha
                ahead = ahead + weight * gc
                prod = prod - weight
                alpha_s[name, i] = alpha
                gc_s[name, i] = gc
            gain_s[name] = prod
            offset_s[name] = ahead
        return carry

    lax.fori_loop(0, (total + LOCAL_WIDE - 1) // LOCAL_WIDE, local_pass, 0)

    def scan_pass(t, carry):
        trans = jnp.ones((1, PIX), f32)
        gains, offsets = [], []
        for b in range(blocks):
            name = t * blocks + b
            alive = b < count_ref[t]
            gains.append(jnp.where(alive, gain_s[name], 1.0))
            offsets.append(jnp.where(alive, offset_s[name], 0.0))
        for b in range(blocks):
            before, whole = scan_before(gains[b], row)
            gain_s[t * blocks + b] = before * trans
            trans = trans * whole
        incoming = jnp.zeros((1, PIX), f32)
        for b in reversed(range(blocks)):
            behind, incoming = scan_behind(gains[b], offsets[b], row, incoming)
            offset_s[t * blocks + b] = behind
        return carry

    lax.fori_loop(0, tiles, scan_pass, 0, unroll=4)

    def grad_pass(k, carry):
        for w in range(GRAD_WIDE):
            name = live[k * GRAD_WIDE + w]
            t, b = name // blocks, name % blocks
            prod = gain_s[name]
            weights = []
            for i in range(steps):
                weight = prod * alpha_s[name, i]
                prod = prod - weight
                weights.append(weight)
            behind = offset_s[name]
            hits = []
            for i in reversed(range(steps)):
                diff = gc_s[name, i] - behind
                hits.append(weights[i] * diff)
                behind = behind + alpha_s[name, i] * diff
            w2 = split_stack(weights)
            h2 = split_stack(hits[::-1])
            head = features[name, 18:21]
            tail = features[name, 24:27]
            colour = jnp.concatenate(
                [
                    jnp.concatenate([head, tail, jnp.zeros((2, BLOCK), f32)], axis=0),
                    jnp.concatenate([head, jnp.zeros((5, BLOCK), f32)], axis=0),
                ],
                axis=1,
            ).astype(bf16)
            image_s[t] += jnp.dot(colour, w2, preferred_element_type=f32)
            got = lax.dot_general(
                up_rows[t].astype(bf16), w2, (((1,), (1,)), ((), ())), preferred_element_type=f32
            )
            colour_grads[t, :, b, :] = got[0:3, :BLOCK] + got[0:3, BLOCK:] + got[3:6, :BLOCK]
            got = lax.dot_general(
                monomials, h2, (((1,), (1,)), ((), ())), preferred_element_type=f32
            )
            moments[t, :, b, :] = got[:, :BLOCK] + got[:, BLOCK:]
        return carry

    lax.fori_loop(0, (total + GRAD_WIDE - 1) // GRAD_WIDE, grad_pass, 0)

    def finish(t, carry):
        image_ref[t] = image_s[t, 0:3] + image_s[t, 3:6]
        alive = block_row < count_ref[t]
        sum_h, sum_x, sum_y, sum_xx, sum_xy, sum_yy = [
            jnp.where(alive, moments[t, m], 0.0) for m in range(6)
        ]
        mid_u, mid_v = middle(t)
        off_u = mid_u - slots_ref[t, 0]
        off_v = mid_v - slots_ref[t, 1]
        con_a, con_b, con_c = (slots_ref[t, 2], slots_ref[t, 3], slots_ref[t, 4])
        sum_u = sum_x + off_u * sum_h
        sum_v = sum_y + off_v * sum_h
        grads_ref[t, 0] = con_a * sum_u + con_b * sum_v
        grads_ref[t, 1] = con_b * sum_u + con_c * sum_v
        grads_ref[t, 2] = -0.5 * (sum_xx + off_u * (sum_x + sum_u))
        grads_ref[t, 3] = -(sum_xy + off_v * sum_x + off_u * sum_v)
        grads_ref[t, 4] = -0.5 * (sum_yy + off_v * (sum_y + sum_v))
        grads_ref[t, 5] = sum_h
        for c in range(3):
            grads_ref[t, 6 + c] = jnp.where(alive, colour_grads[t, c], 0.0)
        return carry

    lax.fori_loop(0, tiles, finish, 0, unroll=4)
    gather_all(back_ref, grads_ref, sent_ref, table, table_low, 0)


def params(**kw):
    return pltpu.CompilerParams(vmem_limit_bytes=vmem_bytes, **kw)


def local(gauss_params, wanted, depth_order, block_count, image_grad):
    peers = wanted.shape[1]
    capacity = wanted.shape[2]
    tiles_here, slots = depth_order.shape
    gauss_here = gauss_params.shape[1]
    lines = capacity // LANES
    groups = gauss_here // (ROWS * LANES)
    blocks = slots // BLOCK
    shape = (groups, CHAN, ROWS, LANES)
    index_shape = (groups, ROWS, LANES)
    tables = [
        pltpu.VMEM(((CHAN - LANED) * 64, 512), bf16),
        pltpu.VMEM((FINE * 64, 256), bf16),
    ]

    def exchange(value):
        if lines != ROWS:
            value = value.transpose(0, 2, 1, 3).reshape(peers, lines, CHAN, LANES).transpose(0, 2, 1, 3)
        value = lax.all_to_all(value, "tile", split_axis=0, concat_axis=0, tiled=True)
        if lines != ROWS:
            value = value.transpose(0, 2, 1, 3).reshape(groups, ROWS, CHAN, LANES).transpose(0, 2, 1, 3)
        return value

    def invert(index):
        return pl.pallas_call(
            invert_kernel,
            out_shape=jax.ShapeDtypeStruct(index_shape, jnp.int32),
            compiler_params=params(),
        )(index)

    asked = lax.all_to_all(
        wanted.reshape(peers, lines, LANES), "tile", split_axis=0, concat_axis=0, tiled=True
    ).reshape(index_shape)
    projected = pl.pallas_call(
        project_kernel,
        out_shape=[
            jax.ShapeDtypeStruct(shape, f32),
            jax.ShapeDtypeStruct(((CHAN - LANED) * 64, 512), bf16),
            jax.ShapeDtypeStruct((FINE * 64, 256), bf16),
        ],
        scratch_shapes=[pltpu.VMEM((PARAMS, ROWS, LANES), f32)],
        compiler_params=params(),
    )(gauss_params)
    order = (
        depth_order.reshape(tiles_here, blocks, ROWS, BLOCK // ROWS)
        .transpose(0, 1, 3, 2)
        .reshape(tiles_here, blocks, BLOCK)
    )
    order_back = invert(order)
    outgoing = pl.pallas_call(
        gather_kernel,
        out_shape=jax.ShapeDtypeStruct(shape, f32),
        compiler_params=params(),
    )(asked, *projected)
    arrived = exchange(outgoing)
    asked_back = invert(asked)
    first_tile = (lax.axis_index("tile") * tiles_here).reshape(1).astype(jnp.int32)
    steps = BLOCK // ROWS
    spare = tiles_here * blocks
    image, sent = pl.pallas_call(
        blend_kernel,
        in_specs=[
            pl.BlockSpec(memory_space=pltpu.SMEM),
            pl.BlockSpec(memory_space=pltpu.SMEM),
            pl.BlockSpec(memory_space=pltpu.VMEM),
            pl.BlockSpec(memory_space=pltpu.VMEM),
            pl.BlockSpec(memory_space=pltpu.VMEM),
            pl.BlockSpec(memory_space=pltpu.VMEM),
        ],
        out_shape=[
            jax.ShapeDtypeStruct((tiles_here, 3, PIX), f32),
            jax.ShapeDtypeStruct(shape, f32),
        ],
        scratch_shapes=tables
        + [
            pltpu.VMEM((tiles_here, CHAN, blocks, BLOCK), f32),
            pltpu.VMEM((tiles_here, CHAN, blocks, BLOCK), f32),
            pltpu.SMEM((spare + LOCAL_WIDE,), jnp.int32),
            pltpu.VMEM((spare + 1, 32, BLOCK), f32),
            pltpu.VMEM((tiles_here + 1, 32, PIX), f32),
            pltpu.VMEM((tiles_here + 1, ROWS, PIX), f32),
            pltpu.VMEM((spare + 1, steps, ROWS, PIX), f32),
            pltpu.VMEM((spare + 1, steps, ROWS, PIX), f32),
            pltpu.VMEM((spare + 1, ROWS, PIX), f32),
            pltpu.VMEM((spare + 1, ROWS, PIX), f32),
            pltpu.VMEM((tiles_here + 1, ROWS, PIX), f32),
            pltpu.VMEM((tiles_here + 1, ROWS, blocks, BLOCK), f32),
            pltpu.VMEM((tiles_here + 1, 3, blocks, BLOCK), f32),
        ],
        compiler_params=params(),
    )(block_count, first_tile, order, order_back, arrived, image_grad)
    returned = exchange(sent)
    param_grads = pl.pallas_call(
        return_kernel,
        out_shape=jax.ShapeDtypeStruct(gauss_params.shape, f32),
        scratch_shapes=tables
        + [
            pltpu.VMEM(shape, f32),
            pltpu.VMEM((PARAMS, ROWS, LANES), f32),
            pltpu.VMEM((PARAMS, ROWS, LANES), f32),
        ],
        compiler_params=params(),
    )(asked_back, returned, gauss_params)
    return (image, param_grads)


def solution(mesh):
    placed = (
        P(None, ("groups", "tile")),
        P(("groups", "tile"), None, None),
        P(("groups", "tile"), None),
        P(("groups", "tile")),
        P(("groups", "tile"), None, None),
    )
    return jax.shard_map(
        local,
        mesh=mesh,
        in_specs=placed,
        out_specs=(P(("groups", "tile"), None, None), P(None, ("groups", "tile"))),
        check_vma=False,
    )
```

```python
import jax
import jax.numpy as jnp
from jax import lax
from jax.experimental import pallas as pl
from jax.experimental.pallas import tpu as pltpu
from jax.sharding import PartitionSpec as P

BLOCK = 128
PIX = 256
LANES = 128
ROWS = 8
CHAN = 9
PARAMS = 14
LANED = 3
AT_ONCE = 8
AT_ONCE_BACK = 4
FINE = 2
LOCAL_WIDE = 16
GRAD_WIDE = 8

focal = 1000.0
center_u = 512.0
center_v = 512.0
dilate = 0.3
tile_row = 64
log_floor = -200.0
vmem_bytes = 56 * 1024 * 1024

f32 = jnp.float32
bf16 = jnp.bfloat16


def pieces(value, count):
    out = []
    for _ in range(count - 1):
        head = value.astype(bf16)
        out.append(head)
        value = value - head.astype(f32)
    out.append(value.astype(bf16))
    return out


def fill_table(read, table, table_low, fine):
    for c in range(CHAN - LANED):
        wide = jnp.concatenate([read(LANED + c, 0), read(LANED + c, 1)], axis=1)
        part = pieces(wide, 3 if c < fine else 2)
        rows = pl.ds(c * 64, 64)
        table[rows, 0:256] = part[0]
        table[rows, 256:512] = part[1]
        if c < fine:
            table_low[rows, :] = part[2]


def pick(index, table, table_low, fine):
    column = (index & 127) | ((index >> 13) << 7)
    row = (index >> 7) & 63
    places = lax.broadcasted_iota(jnp.int32, (256, 256), 0).astype(f32).astype(bf16)
    column = jnp.broadcast_to(column.astype(f32).astype(bf16), (256, 256))
    chosen = jnp.where(column == places, bf16(1), bf16(0))
    row_hit = jnp.broadcast_to(row, (64, 256)) == lax.broadcasted_iota(jnp.int32, (64, 256), 0)
    both = jnp.dot(
        table[...], jnp.concatenate([chosen, chosen], axis=0), preferred_element_type=f32
    )
    if fine:
        low = jnp.dot(table_low[...], chosen, preferred_element_type=f32)
    out = []
    for c in range(CHAN - LANED):
        mine = both[c * 64 : c * 64 + 64]
        if c < fine:
            mine = mine + low[c * 64 : c * 64 + 64]
        out.append(jnp.sum(jnp.where(row_hit, mine, 0.0), axis=0, keepdims=True))
    return out


def gather_all(index_ref, in_ref, out_ref, table, table_low, fine, beside=None, at_once=AT_ONCE, filled=False):
    groups = in_ref.shape[0]
    quarter = groups // (ROWS // 2)
    if not filled:
        fill_table(lambda c, half: read_half(in_ref, c, half), table, table_low, fine)

    def one(t):
        whole = index_ref[t]
        row, column = whole >> 7, whole & 127
        found = [jnp.zeros((ROWS, LANES), f32) for _ in range(LANED)]
        for half in range(ROWS // 2):
            for q in range(half * quarter, half * quarter + quarter):
                for s in range(ROWS):
                    hit = row == q * ROWS + s
                    for c in range(LANED):
                        line = jnp.broadcast_to(in_ref[q, c, s : s + 1, :], (ROWS, LANES))
                        found[c] = jnp.where(
                            hit, jnp.take_along_axis(line, column, axis=1), found[c]
                        )
            index = jnp.concatenate(
                [index_ref[t, 2 * half : 2 * half + 1, :], index_ref[t, 2 * half + 1 : 2 * half + 2, :]],
                axis=1,
            )
            for c, line in enumerate(pick(index, table, table_low, fine)):
                out_ref[t, LANED + c, 2 * half : 2 * half + 1, :] = line[:, :LANES]
                out_ref[t, LANED + c, 2 * half + 1 : 2 * half + 2, :] = line[:, LANES:]
        for c in range(LANED):
            out_ref[t, c] = found[c]

    def step(k, carry):
        for u in range(at_once):
            if beside is not None:
                beside(jnp.maximum(k - 1, 0) * at_once + u)
        for u in range(at_once):
            one(k * at_once + u)
        return carry

    if beside is not None:
        for u in range(at_once):
            out_ref[u] = jnp.zeros_like(out_ref[u])
    lax.fori_loop(0, groups // at_once, step, 0)
    if beside is not None:
        for u in range(at_once):
            beside(groups - at_once + u)


def invert_kernel(index_ref, out_ref):
    place = lax.broadcasted_iota(jnp.int32, (LANES, LANES), 0)
    lane = lax.broadcasted_iota(jnp.int32, (LANES, LANES), 1).astype(f32)

    def step(t, total):
        for s in range(ROWS):
            line = index_ref[t, s : s + 1, :]
            row_hit = jnp.broadcast_to(line >> 7, (LANES, LANES)) == place
            column_hit = jnp.broadcast_to(line & 127, (LANES, LANES)) == place
            here = (t * ROWS + s).astype(f32)
            left = jnp.concatenate(
                [jnp.where(row_hit, here, 0.0).astype(bf16), jnp.where(row_hit, lane, 0.0).astype(bf16)],
                axis=0,
            )
            right = jnp.where(column_hit, 1.0, 0.0).astype(bf16)
            total = total + lax.dot_general(
                left, right, (((1,), (1,)), ((), ())), preferred_element_type=f32
            )
        return total

    total = lax.fori_loop(0, index_ref.shape[0], step, jnp.zeros((2 * LANES, LANES), f32))
    value = (total[:LANES] * float(LANES) + total[LANES:]).astype(jnp.int32)
    for t in range(index_ref.shape[0]):
        out_ref[t] = value[t * ROWS : t * ROWS + ROWS]


def project_core(raw):
    pos_x, pos_y, depth = (raw[0], raw[1], raw[2])
    scale_x, scale_y, scale_z = (jnp.exp(raw[3]), jnp.exp(raw[4]), jnp.exp(raw[5]))
    norm_inv = 1.0 / jnp.sqrt(raw[6] * raw[6] + raw[7] * raw[7] + raw[8] * raw[8] + raw[9] * raw[9])
    q_real, q_one, q_two, q_three = (
        raw[6] * norm_inv,
        raw[7] * norm_inv,
        raw[8] * norm_inv,
        raw[9] * norm_inv,
    )
    rot = [
        [
            1.0 - 2.0 * (q_two * q_two + q_three * q_three),
            2.0 * (q_one * q_two - q_real * q_three),
            2.0 * (q_one * q_three + q_real * q_two),
        ],
        [
            2.0 * (q_one * q_two + q_real * q_three),
            1.0 - 2.0 * (q_one * q_one + q_three * q_three),
            2.0 * (q_two * q_three - q_real * q_one),
        ],
        [
            2.0 * (q_one * q_three - q_real * q_two),
            2.0 * (q_two * q_three + q_real * q_one),
            1.0 - 2.0 * (q_one * q_one + q_two * q_two),
        ],
    ]
    scales = [scale_x, scale_y, scale_z]
    mixed = [[rot[i][k] * scales[k] for k in range(3)] for i in range(3)]
    cov = [
        [
            mixed[i][0] * mixed[j][0] + mixed[i][1] * mixed[j][1] + mixed[i][2] * mixed[j][2]
            for j in range(3)
        ]
        for i in range(3)
    ]
    depth_inv = 1.0 / depth
    jac_uu = focal * depth_inv
    jac_uz = -jac_uu * (pos_x * depth_inv)
    jac_vv = jac_uu
    jac_vz = -jac_uu * (pos_y * depth_inv)
    upper = [jac_uu * cov[0][k] + jac_uz * cov[2][k] for k in range(3)]
    lower = [jac_vv * cov[1][k] + jac_vz * cov[2][k] for k in range(3)]
    first = upper[0] * jac_uu + upper[2] * jac_uz + dilate
    cross = upper[1] * jac_vv + upper[2] * jac_vz
    second = lower[1] * jac_vv + lower[2] * jac_vz + dilate
    det_inv = 1.0 / (first * second - cross * cross)
    return [
        focal * pos_x * depth_inv + center_u,
        focal * pos_y * depth_inv + center_v,
        second * det_inv,
        -cross * det_inv,
        first * det_inv,
    ]


def sigmoid(x):
    return 1.0 / (1.0 + jnp.exp(-x))


def project_kernel(params_ref, out_ref, table, table_low, raw):
    def step(t, carry):
        for s in range(ROWS):
            raw[:, s, :] = params_ref[:, pl.ds(pl.multiple_of((t * ROWS + s) * LANES, LANES), LANES)]
        rows = project_core([raw[k] for k in range(10)])
        for c in range(5):
            out_ref[t, c] = rows[c]
        out_ref[t, 5] = sigmoid(raw[10])
        for c in range(3):
            out_ref[t, 6 + c] = raw[11 + c]
        return carry

    lax.fori_loop(0, out_ref.shape[0], step, 0)
    fill_table(lambda c, half: read_half(out_ref, c, half), table, table_low, FINE)


def read_half(ref, c, half):
    groups = ref.shape[0] // 2
    return jnp.concatenate([ref[half * groups + q, c] for q in range(groups)], axis=0)


def gather_kernel(index_ref, in_ref, table, table_low, out_ref):
    gather_all(index_ref, in_ref, out_ref, table, table_low, FINE, filled=True)


def return_kernel(index_ref, grads_ref, params_ref, out_ref, table, table_low, summed, raw, stage):
    def back(t):
        for s in range(ROWS):
            raw[:, s, :] = params_ref[:, pl.ds(pl.multiple_of((t * ROWS + s) * LANES, LANES), LANES)]
        _, pull = jax.vjp(project_core, [raw[k] for k in range(10)])
        core = pull([summed[t, c] for c in range(5)])[0]
        for k in range(10):
            stage[k] = core[k]
        stage[10] = summed[t, 5] * sigmoid(-raw[10])
        for c in range(3):
            stage[11 + c] = summed[t, 6 + c]
        for s in range(ROWS):
            out_ref[:, pl.ds(pl.multiple_of((t * ROWS + s) * LANES, LANES), LANES)] = stage[:, s, :]

    gather_all(index_ref, grads_ref, summed, table, table_low, 0, back, AT_ONCE_BACK)


def scan_before(value, row):
    total = value
    for shift in (1, 2, 4):
        total = total * jnp.where(row >= shift, pltpu.roll(total, shift, 0), 1.0)
    before = jnp.where(row >= 1, pltpu.roll(total, 1, 0), 1.0)
    return before, total[ROWS - 1 : ROWS, :]


def scan_behind(gain, offset, row, incoming):
    for shift in (1, 2, 4):
        inside = row < ROWS - shift
        offset = offset + gain * jnp.where(inside, pltpu.roll(offset, ROWS - shift, 0), 0.0)
        gain = gain * jnp.where(inside, pltpu.roll(gain, ROWS - shift, 0), 1.0)
    value = offset + gain * incoming
    behind = jnp.where(row < ROWS - 1, pltpu.roll(value, ROWS - 1, 0), incoming)
    return behind, value[0:1, :]


def two_rows(value):
    head = value.astype(bf16)
    return head, (value - head.astype(f32)).astype(bf16)


def split_stack(values):
    head, tail = two_rows(jnp.concatenate(values, axis=0))
    return jnp.concatenate([head, tail], axis=0)


def blend_kernel(
    count_ref,
    first_ref,
    order_ref,
    back_ref,
    arrived_ref,
    upstream_ref,
    image_ref,
    sent_ref,
    table,
    table_low,
    slots_ref,
    grads_ref,
    live,
    features,
    basis,
    up_rows,
    alpha_s,
    gc_s,
    gain_s,
    offset_s,
    image_s,
    moments,
    colour_grads,
):
    gather_all(order_ref, arrived_ref, slots_ref, table, table_low, FINE)
    tiles, _, blocks, _ = slots_ref.shape
    steps = BLOCK // ROWS
    spare = tiles * blocks
    pixel = lax.broadcasted_iota(jnp.int32, (1, PIX), 1)
    x = (pixel & 15).astype(f32) - 7.5
    y = (pixel >> 4).astype(f32) - 7.5
    row = lax.broadcasted_iota(jnp.int32, (ROWS, PIX), 0)
    block_row = lax.broadcasted_iota(jnp.int32, (blocks, BLOCK), 0)
    six = jnp.concatenate([jnp.ones_like(x), x, y, x * x, x * y, y * y], axis=0)
    power_basis = jnp.concatenate([six, six, six, jnp.zeros((14, PIX), f32)], axis=0).astype(bf16)
    monomials = jnp.concatenate([six, jnp.zeros((2, PIX), f32)], axis=0).astype(bf16)

    def middle(t):
        tile = first_ref[0] + t
        return (
            ((tile % tile_row) * 16 + 8).astype(f32),
            ((tile // tile_row) * 16 + 8).astype(f32),
        )

    basis[...] = jnp.zeros_like(basis)
    features[pl.ds(spare, 1)] = jnp.zeros((1, 32, BLOCK), f32)
    features[:, 27:32, :] = jnp.zeros((spare + 1, 5, BLOCK), f32)
    up_rows[pl.ds(tiles, 1)] = jnp.zeros((1, ROWS, PIX), f32)
    image_s[...] = jnp.zeros_like(image_s)

    def prepare(t, total):
        up = upstream_ref[t]
        up_head = up.astype(bf16).astype(f32)
        up_tail = up - up_head
        basis[t, 18:21, :] = up_head
        basis[t, 21:24, :] = up_tail
        basis[t, 24:27, :] = up_head
        up_rows[t] = jnp.concatenate([up_head, up_tail, jnp.zeros((2, PIX), f32)], axis=0)
        mid_u, mid_v = middle(t)
        off_u = mid_u - slots_ref[t, 0]
        off_v = mid_v - slots_ref[t, 1]
        con_a, con_b, con_c = (slots_ref[t, 2], slots_ref[t, 3], slots_ref[t, 4])
        log_op = jnp.maximum(jnp.log(slots_ref[t, 5]), log_floor)
        side_u = con_a * off_u + con_b * off_v
        side_v = con_b * off_u + con_c * off_v
        coefs = [
            log_op - 0.5 * (off_u * side_u + off_v * side_v),
            -side_u,
            -side_v,
            -0.5 * con_a,
            -con_b,
            -0.5 * con_c,
        ]
        here = pl.ds(t * blocks, blocks)
        for m, coef in enumerate(coefs):
            for k, part in enumerate(pieces(coef, 3)):
                features[here, 6 * k + m, :] = part.astype(f32)
        for c in range(3):
            head, tail = two_rows(slots_ref[t, 6 + c])
            features[here, 18 + c, :] = head.astype(f32)
            features[here, 21 + c, :] = head.astype(f32)
            features[here, 24 + c, :] = tail.astype(f32)
        for b in range(blocks):
            live[total] = t * blocks + b
            total = total + (b < count_ref[t]).astype(jnp.int32)
        return total

    total = lax.fori_loop(0, tiles, prepare, jnp.int32(0), unroll=4)
    for k in range(LOCAL_WIDE):
        live[total + k] = spare

    def local_pass(k, carry):
        for w in range(LOCAL_WIDE):
            name = live[k * LOCAL_WIDE + w]
            block = features[name].astype(bf16)
            power = lax.dot_general(
                block, power_basis, (((0,), (0,)), ((), ())), preferred_element_type=f32
            )
            shade = lax.dot_general(
                block,
                basis[name // blocks].astype(bf16),
                (((0,), (0,)), ((), ())),
                preferred_element_type=f32,
            )
            prod = jnp.ones((ROWS, PIX), f32)
            ahead = jnp.zeros((ROWS, PIX), f32)
            for i in range(steps):
                alpha = jnp.exp(power[i * ROWS : i * ROWS + ROWS])
                gc = shade[i * ROWS : i * ROWS + ROWS]
                weight = prod * alpha
                ahead = ahead + weight * gc
                prod = prod - weight
                alpha_s[name, i] = alpha
                gc_s[name, i] = gc
            gain_s[name] = prod
            offset_s[name] = ahead
        return carry

    lax.fori_loop(0, (total + LOCAL_WIDE - 1) // LOCAL_WIDE, local_pass, 0)

    def scan_pass(t, carry):
        trans = jnp.ones((1, PIX), f32)
        gains, offsets = [], []
        for b in range(blocks):
            name = t * blocks + b
            alive = b < count_ref[t]
            gains.append(jnp.where(alive, gain_s[name], 1.0))
            offsets.append(jnp.where(alive, offset_s[name], 0.0))
        for b in range(blocks):
            before, whole = scan_before(gains[b], row)
            gain_s[t * blocks + b] = before * trans
            trans = trans * whole
        incoming = jnp.zeros((1, PIX), f32)
        for b in reversed(range(blocks)):
            behind, incoming = scan_behind(gains[b], offsets[b], row, incoming)
            offset_s[t * blocks + b] = behind
        return carry

    lax.fori_loop(0, tiles, scan_pass, 0, unroll=4)

    def grad_pass(k, carry):
        for w in range(GRAD_WIDE):
            name = live[k * GRAD_WIDE + w]
            t, b = name // blocks, name % blocks
            prod = gain_s[name]
            weights = []
            for i in range(steps):
                weight = prod * alpha_s[name, i]
                prod = prod - weight
                weights.append(weight)
            behind = offset_s[name]
            hits = []
            for i in reversed(range(steps)):
                diff = gc_s[name, i] - behind
                hits.append(weights[i] * diff)
                behind = behind + alpha_s[name, i] * diff
            w2 = split_stack(weights)
            h2 = split_stack(hits[::-1])
            head = features[name, 18:21]
            tail = features[name, 24:27]
            colour = jnp.concatenate(
                [
                    jnp.concatenate([head, tail, jnp.zeros((2, BLOCK), f32)], axis=0),
                    jnp.concatenate([head, jnp.zeros((5, BLOCK), f32)], axis=0),
                ],
                axis=1,
            ).astype(bf16)
            image_s[t] += jnp.dot(colour, w2, preferred_element_type=f32)
            got = lax.dot_general(
                up_rows[t].astype(bf16), w2, (((1,), (1,)), ((), ())), preferred_element_type=f32
            )
            colour_grads[t, :, b, :] = got[0:3, :BLOCK] + got[0:3, BLOCK:] + got[3:6, :BLOCK]
            got = lax.dot_general(
                monomials, h2, (((1,), (1,)), ((), ())), preferred_element_type=f32
            )
            moments[t, :, b, :] = got[:, :BLOCK] + got[:, BLOCK:]
        return carry

    lax.fori_loop(0, (total + GRAD_WIDE - 1) // GRAD_WIDE, grad_pass, 0)

    def finish(t, carry):
        image_ref[t] = image_s[t, 0:3] + image_s[t, 3:6]
        alive = block_row < count_ref[t]
        sum_h, sum_x, sum_y, sum_xx, sum_xy, sum_yy = [
            jnp.where(alive, moments[t, m], 0.0) for m in range(6)
        ]
        mid_u, mid_v = middle(t)
        off_u = mid_u - slots_ref[t, 0]
        off_v = mid_v - slots_ref[t, 1]
        con_a, con_b, con_c = (slots_ref[t, 2], slots_ref[t, 3], slots_ref[t, 4])
        sum_u = sum_x + off_u * sum_h
        sum_v = sum_y + off_v * sum_h
        grads_ref[t, 0] = con_a * sum_u + con_b * sum_v
        grads_ref[t, 1] = con_b * sum_u + con_c * sum_v
        grads_ref[t, 2] = -0.5 * (sum_xx + off_u * (sum_x + sum_u))
        grads_ref[t, 3] = -(sum_xy + off_v * sum_x + off_u * sum_v)
        grads_ref[t, 4] = -0.5 * (sum_yy + off_v * (sum_y + sum_v))
        grads_ref[t, 5] = sum_h
        for c in range(3):
            grads_ref[t, 6 + c] = jnp.where(alive, colour_grads[t, c], 0.0)
        return carry

    lax.fori_loop(0, tiles, finish, 0, unroll=4)
    gather_all(back_ref, grads_ref, sent_ref, table, table_low, 0)


def params(**kw):
    return pltpu.CompilerParams(vmem_limit_bytes=vmem_bytes, **kw)


def local(gauss_params, wanted, depth_order, block_count, image_grad):
    peers = wanted.shape[1]
    capacity = wanted.shape[2]
    tiles_here, slots = depth_order.shape
    gauss_here = gauss_params.shape[1]
    lines = capacity // LANES
    groups = gauss_here // (ROWS * LANES)
    blocks = slots // BLOCK
    shape = (groups, CHAN, ROWS, LANES)
    index_shape = (groups, ROWS, LANES)
    tables = [
        pltpu.VMEM(((CHAN - LANED) * 64, 512), bf16),
        pltpu.VMEM((FINE * 64, 256), bf16),
    ]

    def exchange(value):
        if lines != ROWS:
            value = value.transpose(0, 2, 1, 3).reshape(peers, lines, CHAN, LANES).transpose(0, 2, 1, 3)
        value = lax.all_to_all(value, "tile", split_axis=0, concat_axis=0, tiled=True)
        if lines != ROWS:
            value = value.transpose(0, 2, 1, 3).reshape(groups, ROWS, CHAN, LANES).transpose(0, 2, 1, 3)
        return value

    def invert(index):
        return pl.pallas_call(
            invert_kernel,
            out_shape=jax.ShapeDtypeStruct(index_shape, jnp.int32),
            compiler_params=params(),
        )(index)

    asked = lax.all_to_all(
        wanted.reshape(peers, lines, LANES), "tile", split_axis=0, concat_axis=0, tiled=True
    ).reshape(index_shape)
    projected = pl.pallas_call(
        project_kernel,
        out_shape=[
            jax.ShapeDtypeStruct(shape, f32),
            jax.ShapeDtypeStruct(((CHAN - LANED) * 64, 512), bf16),
            jax.ShapeDtypeStruct((FINE * 64, 256), bf16),
        ],
        scratch_shapes=[pltpu.VMEM((PARAMS, ROWS, LANES), f32)],
        compiler_params=params(),
    )(gauss_params)
    order = (
        depth_order.reshape(tiles_here, blocks, ROWS, BLOCK // ROWS)
        .transpose(0, 1, 3, 2)
        .reshape(tiles_here, blocks, BLOCK)
    )
    order_back = invert(order)
    outgoing = pl.pallas_call(
        gather_kernel,
        out_shape=jax.ShapeDtypeStruct(shape, f32),
        compiler_params=params(),
    )(asked, *projected)
    arrived = exchange(outgoing)
    asked_back = invert(asked)
    first_tile = (lax.axis_index("tile") * tiles_here).reshape(1).astype(jnp.int32)
    steps = BLOCK // ROWS
    spare = tiles_here * blocks
    image, sent = pl.pallas_call(
        blend_kernel,
        in_specs=[
            pl.BlockSpec(memory_space=pltpu.SMEM),
            pl.BlockSpec(memory_space=pltpu.SMEM),
            pl.BlockSpec(memory_space=pltpu.VMEM),
            pl.BlockSpec(memory_space=pltpu.VMEM),
            pl.BlockSpec(memory_space=pltpu.VMEM),
            pl.BlockSpec(memory_space=pltpu.VMEM),
        ],
        out_shape=[
            jax.ShapeDtypeStruct((tiles_here, 3, PIX), f32),
            jax.ShapeDtypeStruct(shape, f32),
        ],
        scratch_shapes=tables
        + [
            pltpu.VMEM((tiles_here, CHAN, blocks, BLOCK), f32),
            pltpu.VMEM((tiles_here, CHAN, blocks, BLOCK), f32),
            pltpu.SMEM((spare + LOCAL_WIDE,), jnp.int32),
            pltpu.VMEM((spare + 1, 32, BLOCK), f32),
            pltpu.VMEM((tiles_here + 1, 32, PIX), f32),
            pltpu.VMEM((tiles_here + 1, ROWS, PIX), f32),
            pltpu.VMEM((spare + 1, steps, ROWS, PIX), f32),
            pltpu.VMEM((spare + 1, steps, ROWS, PIX), f32),
            pltpu.VMEM((spare + 1, ROWS, PIX), f32),
            pltpu.VMEM((spare + 1, ROWS, PIX), f32),
            pltpu.VMEM((tiles_here + 1, ROWS, PIX), f32),
            pltpu.VMEM((tiles_here + 1, ROWS, blocks, BLOCK), f32),
            pltpu.VMEM((tiles_here + 1, 3, blocks, BLOCK), f32),
        ],
        compiler_params=params(),
    )(block_count, first_tile, order, order_back, arrived, image_grad)
    returned = exchange(sent)
    param_grads = pl.pallas_call(
        return_kernel,
        out_shape=jax.ShapeDtypeStruct(gauss_params.shape, f32),
        scratch_shapes=tables
        + [
            pltpu.VMEM(shape, f32),
            pltpu.VMEM((PARAMS, ROWS, LANES), f32),
            pltpu.VMEM((PARAMS, ROWS, LANES), f32),
        ],
        compiler_params=params(),
    )(asked_back, returned, gauss_params)
    return (image, param_grads)


def solution(mesh):
    placed = (
        P(None, ("groups", "tile")),
        P(("groups", "tile"), None, None),
        P(("groups", "tile"), None),
        P(("groups", "tile")),
        P(("groups", "tile"), None, None),
    )
    return jax.shard_map(
        local,
        mesh=mesh,
        in_specs=placed,
        out_specs=(P(("groups", "tile"), None, None), P(None, ("groups", "tile"))),
        check_vma=False,
    )
```
